256 devices in a mesh: rows: 32 (over y, z), cols: 8 (over x, core).
Axes of the slice: x: 4, y: 4, z: 8, core: 2. Of those that a mesh axis runs over, the one named last changes fastest.
Arguments:
- x_feat: bfloat16 [64, 65536], P(None, ('rows', 'cols')), may hold values from -24 to 24
- y_feat: bfloat16 [64, 65536], P(None, ('cols', 'rows')), may hold values from -24 to 24
- log_a: float32 [65536], P(('rows', 'cols')), may hold values from -8 to 8
- log_b: float32 [65536], P(('cols', 'rows')), may hold values from -8 to 8
- g_init: float32 [65536], P('cols'), may hold values from -3 to 3
Outputs:
- f_pot: float32 [65536], P('rows')
- g_pot: float32 [65536], P('cols')
The draws below stay inside these ranges and needn't reach their ends.
All inputs are finite; a program needn't handle non-finite values.
Results may differ from the reference program's by a relative error of at most 0.0018.
Values may be sent and summed in bfloat16 or wider, within the bound.
No kernel may reach another device: no remote copies, remote signals or barrier semaphores. Data moves between devices by JAX's collectives and lax.ppermute only.
A program may use at most 64 MiB of HBM per device.

```python
import math
import jax
import jax.numpy as jnp
from jax import lax

FEAT = 64
N1 = 65536
N2 = 65536


def atlas_pair(key, lower_log, upper_log):
    key = jax.random.fold_in(key, 11)
    split_keys = jax.random.split(key, 5)
    big_count = min(64, N1 // 8)
    copy_count = big_count // 2
    flat_count = 16
    scales = jnp.exp(jax.random.uniform(split_keys[0], (N1,), jnp.float32, lower_log, upper_log))
    big_cols = jax.random.permutation(split_keys[1], N1)[:big_count]
    scales = scales.at[big_cols].set(4.0)
    normal_base = jax.random.truncated_normal(split_keys[2], -6.0, 6.0, (FEAT, N1), jnp.float32)
    x_vals = normal_base * scales[None, :]
    x_vals = x_vals.at[0, big_cols[0]].set(24.0)
    x_vals = x_vals.at[1, big_cols[0]].set(-24.0)
    x_vals = x_vals.astype(jnp.bfloat16)
    targets = jax.random.permutation(split_keys[3], N2)[:copy_count + flat_count]
    y_vals = jax.random.truncated_normal(split_keys[4], -6.0, 6.0, (FEAT, N2), jnp.float32)
    copied = x_vals[:, big_cols[:copy_count]].astype(jnp.float32)
    y_vals = y_vals.at[:, targets[:copy_count]].set(copied)
    y_vals = y_vals.at[:, targets[copy_count:]].set(6.0)
    return (x_vals, y_vals.astype(jnp.bfloat16))


def draw_x_feat(key, part):
    x_vals, y_vals = atlas_pair(key, math.log(0.5), math.log(2.0))
    return x_vals


def draw_y_feat(key, part):
    x_vals, y_vals = atlas_pair(key, math.log(0.5), math.log(2.0))
    return y_vals


def block_levels(rng, shape, pieces, least, largest):
    gain = 1.0
    for position, shards_of in pieces:
        heights = jax.random.uniform(jax.random.fold_in(jax.random.fold_in(rng, 6), position), (shards_of,), jnp.float32, least / len(pieces), largest / len(pieces))
        gain = gain * jnp.repeat(jnp.exp(heights), shape[position] // shards_of).reshape((-1,) + (1,) * (len(shape) - 1 - position))
    return gain


def gaussian(own_key, extent, scale, limit, pieces=(), held_as=jnp.bfloat16):
    gain = block_levels(own_key, extent, pieces, -0.22, 0.18) if pieces else 1.0
    values = jax.random.normal(own_key, extent, jnp.float32) * scale * gain
    return jnp.minimum(jnp.maximum(values, -limit), limit).astype(held_as)


def setup_inputs(seed: int = 0) -> dict:
    streams_of = jax.random.split(jax.random.key(seed), 6)
    return {
        "x_feat": draw_x_feat(jax.random.fold_in(streams_of[5], 71), 0),
        "y_feat": draw_y_feat(jax.random.fold_in(streams_of[5], 71), 0),
        "log_a": gaussian(streams_of[2], (N1,), 2.0, 8.0, ((0, 256),), jnp.float32),
        "log_b": gaussian(streams_of[3], (N2,), 2.0, 8.0, ((0, 256),), jnp.float32),
        "g_init": gaussian(streams_of[4], (N2,), 0.5, 3.0, ((0, 8),), jnp.float32),
    }


EPS = 0.05


def cost_tile(xb, nxb, y, ny, feat):
    inner = lax.dot_general(xb, y, ((((0,), (0,))), ((), ())), preferred_element_type=jnp.float32)
    return (nxb[:, None] + ny[None, :] - 2.0 * inner) / feat


def reference(x_feat, y_feat, log_a, log_b, g_init):
    feat = x_feat.shape[0]
    nx = jnp.sum(jnp.square(x_feat.astype(jnp.float32)), axis=0)
    ny = jnp.sum(jnp.square(y_feat.astype(jnp.float32)), axis=0)
    total = x_feat.shape[1]
    block = min(1024, total)
    count = total // block
    xs = jnp.transpose(x_feat.reshape(feat, count, block), (1, 0, 2))
    nxs = nx.reshape(count, block)

    def row_block(args):
        xb, nxb = args
        cost = cost_tile(xb, nxb, y_feat, ny, feat)
        expo = log_b[None, :] + (g_init[None, :] - cost) / EPS
        top = jnp.max(expo, axis=1)
        return -EPS * (top + jnp.log(jnp.sum(jnp.exp(expo - top[:, None]), axis=1)))

    f_pot = lax.map(row_block, (xs, nxs)).reshape(total)
    fs = f_pot.reshape(count, block)
    las = log_a.reshape(count, block)

    def col_block(carry, args):
        top, acc = carry
        xb, nxb, fb, lab = args
        cost = cost_tile(xb, nxb, y_feat, ny, feat)
        expo = lab[:, None] + (fb[:, None] - cost) / EPS
        new_top = jnp.maximum(top, jnp.max(expo, axis=0))
        acc = acc * jnp.exp(top - new_top) + jnp.sum(jnp.exp(expo - new_top[None, :]), axis=0)
        return (new_top, acc), None

    start = (jnp.full(ny.shape, -jnp.inf, jnp.float32), jnp.zeros(ny.shape, jnp.float32))
    (top, acc), unused = lax.scan(col_block, start, (xs, nxs, fs, las))
    g_pot = -EPS * (top + jnp.log(acc))
    return f_pot, g_pot
```

```python
import functools

import jax
import jax.numpy as jnp
from jax import lax
from jax.experimental import pallas as pl
from jax.experimental.pallas import tpu as pltpu
from jax.sharding import PartitionSpec as P

EPS = 0.05
LOG2E = 1.4426950408889634
LN2 = 0.6931471805599453
BF16 = jnp.bfloat16
F32 = jnp.float32
PIECE = 256
EXTRA = 16
DEPTH = 256
LOW = -1e30
VMEM_LIMIT = 56 * 1024 * 1024


def split3(v):
    high = v.astype(BF16).astype(F32)
    rest = v - high
    mid = rest.astype(BF16).astype(F32)
    return high, mid, rest - mid


def wide(ref, row):
    pair = ref[pl.ds(row, 2), :]
    return jnp.concatenate([pair[0:1], pair[1:2]], axis=1)


def rows_of(terms, count, width):
    row = lax.broadcasted_iota(jnp.int32, (count, width), 0)
    out = jnp.zeros((count, width), F32)
    for index, term in enumerate(terms):
        out = jnp.where(row == index, term, out)
    return out


def pack_kernel(x_ref, y_ref, la_ref, lb_ref, g_ref, xo_ref, yo_ref):
    feat = x_ref.shape[0]
    la = wide(la_ref, 0) * LOG2E
    y = y_ref[...].astype(F32)
    ny = jnp.sum(y * y, axis=0, keepdims=True)
    mine = lax.axis_index("rows")
    g = wide(g_ref, 2 * mine)
    own = (wide(lb_ref, 0) + (g - ny / feat) / EPS) * LOG2E
    one = jnp.ones((1, PIECE), F32)
    x_extra = rows_of(split3(la), EXTRA, PIECE).astype(BF16)
    y_extra = rows_of(split3(own) + (one, one, one), EXTRA, PIECE).astype(BF16)
    for d in range(xo_ref.shape[0]):
        xo_ref[d, 0:feat, :] = x_ref[...]
        xo_ref[d, feat : feat + EXTRA, :] = x_extra
    for d in range(yo_ref.shape[0]):
        yo_ref[d, 0:feat, :] = y_ref[...]
        yo_ref[d, feat : feat + EXTRA, :] = y_extra


def left_side(x_ref, p, extra, scale):
    feat = x_ref.shape[1] - EXTRA
    parts = split3(x_ref[p, 0:feat, :].astype(F32) * scale)
    fill = jnp.zeros((DEPTH - 3 * feat - EXTRA, PIECE), F32)
    return jnp.transpose(jnp.concatenate(parts + (extra, fill), axis=0)).astype(BF16)


def right_side(y_ref, p):
    feat = y_ref.shape[1] - EXTRA
    y = y_ref[p, 0:feat, :]
    extra = y_ref[p, feat : feat + EXTRA, :]
    fill = jnp.zeros((DEPTH - 3 * feat - EXTRA, PIECE), BF16)
    return jnp.concatenate([y, y, y, extra, fill], axis=0)


def dot(a, b):
    return jnp.dot(a, b, preferred_element_type=F32)


IB = 512
JP = 4


def row_kernel(x_ref, y_ref, out_ref, a_ref, s_ref, m_ref, l_ref, *, scale):
    pieces = x_ref.shape[0]
    n = pieces * PIECE
    one = jnp.ones((1, PIECE), F32)
    extra = rows_of((one, one, one), EXTRA, PIECE)
    for p in range(pieces):
        a_ref[p * PIECE : (p + 1) * PIECE, :] = left_side(x_ref, p, extra, scale)
    m_ref[...] = jnp.full(m_ref.shape, LOW, F32)
    l_ref[...] = jnp.zeros(l_ref.shape, F32)
    blocks = n // IB
    steps = blocks * (y_ref.shape[0] // JP)

    def start(t, k):
        base = pl.multiple_of((t % blocks) * IB, IB)
        return dot(a_ref[pl.ds(base, IB), :], right_side(y_ref, (t // blocks) * JP + k))

    def finish(t, slot, r):
        base = pl.multiple_of((t % blocks) * IB + r, 8)
        rows = pl.ds(base, 8)
        vals = [s_ref[slot, r : r + 8, c * 128 : (c + 1) * 128] for c in range(JP * 2)]
        old = m_ref[rows, :]
        top = old
        for v in vals:
            top = jnp.maximum(top, v)
        acc = l_ref[rows, :] * jnp.exp2(old - top)
        for v in vals:
            acc = acc + jnp.exp2(v - top)
        m_ref[rows, :] = top
        l_ref[rows, :] = acc

    def half(t, slot):
        later = jnp.minimum(t + 1, steps - 1)
        for k in range(JP):
            s_ref[1 - slot, :, k * PIECE : (k + 1) * PIECE] = start(later, k)
            for r in range(k * IB // JP, (k + 1) * IB // JP, 8):
                finish(t, slot, r)

    for k in range(JP):
        s_ref[0, :, k * PIECE : (k + 1) * PIECE] = start(0, k)

    def body(u, carry):
        half(2 * u, 0)
        half(2 * u + 1, 1)
        return carry

    lax.fori_loop(0, steps // 2, body, 0)
    for q in range(n // 128):
        mt = jnp.transpose(m_ref[q * 128 : (q + 1) * 128, :])
        lt = jnp.transpose(l_ref[q * 128 : (q + 1) * 128, :])
        top = jnp.max(mt, axis=0, keepdims=True)
        lse = top + jnp.log2(jnp.sum(lt * jnp.exp2(mt - top), axis=0, keepdims=True))
        for d in range(out_ref.shape[0]):
            out_ref[d, q : q + 1, :] = lse


def col_kernel(x_ref, y_ref, lse_ref, f_ref, out_ref, a_ref, s_ref, *, scale):
    pieces, feat = x_ref.shape[0], x_ref.shape[1] - EXTRA
    n = pieces * PIECE
    tiles = y_ref.shape[0]
    part = lse_ref[...]
    top = jnp.max(part, axis=0)
    whole = top + jnp.log2(jnp.sum(jnp.exp2(part - top[None]), axis=0))
    zero = jnp.zeros((1, PIECE), F32)
    for p in range(pieces):
        lse = jnp.concatenate([whole[2 * p : 2 * p + 1], whole[2 * p + 1 : 2 * p + 2]], axis=1)
        x = x_ref[p, 0:feat, :].astype(F32)
        nx = jnp.sum(x * x, axis=0, keepdims=True)
        f = nx / feat - (EPS * LN2) * lse
        f_ref[2 * p : 2 * p + 1, :] = f[:, 0:128]
        f_ref[2 * p + 1 : 2 * p + 2, :] = f[:, 128:256]
        la = jnp.sum(x_ref[p, feat : feat + EXTRA, :].astype(F32), axis=0, keepdims=True)
        extra = rows_of((zero, zero, zero) + split3(la - lse), EXTRA, PIECE)
        a_ref[p * PIECE : (p + 1) * PIECE, :] = left_side(x_ref, p, extra, scale)
    chunk = 512

    def start(t, k):
        return dot(a_ref[k * chunk : (k + 1) * chunk, :], right_side(y_ref, t))

    def fold(s, how):
        return how(s.reshape(s.shape[0] // 8, 8, s.shape[1]), axis=0)

    def half(t, slot, top):
        later = jnp.minimum(t + 1, tiles - 1)
        new = jnp.full((8, PIECE), LOW, F32)
        acc = jnp.zeros((8, PIECE), F32)
        for k in range(n // chunk):
            s = start(later, k)
            s_ref[1 - slot, k * chunk : (k + 1) * chunk, :] = s
            new = jnp.maximum(new, fold(s, jnp.max))
            for r in range(k * chunk, (k + 1) * chunk, 64):
                v = s_ref[slot, r : r + 64, :].reshape(8, 8, PIECE)
                acc = acc + jnp.sum(jnp.exp2(v - top[None]), axis=0)
        peak = jnp.max(top, axis=0, keepdims=True)
        total = jnp.sum(acc * jnp.exp2(top - peak), axis=0, keepdims=True)
        y = y_ref[t, 0:feat, :].astype(F32)
        ny = jnp.sum(y * y, axis=0, keepdims=True)
        u = peak + jnp.log2(total) - ny * (LOG2E / (feat * EPS))
        for d in range(out_ref.shape[0]):
            out_ref[d, pl.ds(2 * t, 1), :] = u[:, 0:128]
            out_ref[d, pl.ds(2 * t + 1, 1), :] = u[:, 128:256]
        return new

    top = jnp.full((8, PIECE), LOW, F32)
    for k in range(n // chunk):
        s = start(0, k)
        s_ref[0, k * chunk : (k + 1) * chunk, :] = s
        top = jnp.maximum(top, fold(s, jnp.max))

    def body(u, top):
        return half(2 * u + 1, 1, half(2 * u, 0, top))

    lax.fori_loop(0, tiles // 2, body, top)


def merge_kernel(u_ref, out_ref):
    u = u_ref[...]
    top = jnp.max(u, axis=0)
    whole = top + jnp.log2(jnp.sum(jnp.exp2(u - top[None]), axis=0))
    for d in range(out_ref.shape[0]):
        out_ref[d] = whole


def last_kernel(u_ref, out_ref):
    u = u_ref[...]
    top = jnp.max(u, axis=0)
    out_ref[...] = (top + jnp.log2(jnp.sum(jnp.exp2(u - top[None]), axis=0))) * (-EPS * LN2)


def call(kernel, outs, args, scratch=(), name=None):
    vmem = pl.BlockSpec(memory_space=pltpu.VMEM)
    return pl.pallas_call(
        kernel,
        out_shape=outs,
        in_specs=[vmem] * len(args),
        out_specs=jax.tree.map(lambda _: vmem, outs),
        scratch_shapes=list(scratch),
        compiler_params=pltpu.CompilerParams(vmem_limit_bytes=VMEM_LIMIT),
        name=name,
    )(*args)


def local(groups, x_feat, y_feat, log_a, log_b, g_init):
    z_groups, y_groups, nc = groups
    ny_, nz = len(z_groups), len(y_groups)
    feat, piece = x_feat.shape
    scale = 2.0 * LOG2E / (feat * EPS)
    shape = jax.ShapeDtypeStruct
    depth = feat + EXTRA
    xo, yo = call(
        pack_kernel,
        [shape((nc, depth, piece), BF16), shape((nz, depth, piece), BF16)],
        (
            x_feat,
            y_feat,
            log_a.reshape(-1, 128),
            log_b.reshape(-1, 128),
            g_init.reshape(-1, 128),
        ),
        name="pack",
    )
    xs = lax.all_to_all(xo, "cols", 0, 0)
    yz = lax.all_to_all(yo, "rows", 0, 0, axis_index_groups=z_groups)
    ys = lax.all_to_all(
        jnp.broadcast_to(yz[None], (ny_,) + yz.shape), "rows", 0, 0, axis_index_groups=y_groups
    ).reshape(ny_ * nz, depth, piece)
    n, m = nc * piece, ny_ * nz * piece
    lse = call(
        functools.partial(row_kernel, scale=scale),
        shape((nc, n // 128, 128), F32),
        (xs, ys),
        [
            pltpu.VMEM((n, DEPTH), BF16),
            pltpu.VMEM((2, IB, JP * PIECE), F32),
            pltpu.VMEM((n, 128), F32),
            pltpu.VMEM((n, 128), F32),
        ],
        name="row_pass",
    )
    parts = lax.all_to_all(lse, "cols", 0, 0)
    f, u = call(
        functools.partial(col_kernel, scale=scale),
        [shape((n // 128, 128), F32), shape((nz, m // 128, 128), F32)],
        (xs, ys, parts),
        [pltpu.VMEM((n, DEPTH), BF16), pltpu.VMEM((2, n, PIECE), F32)],
        name="col_pass",
    )
    u = lax.all_to_all(u, "rows", 0, 0, axis_index_groups=z_groups)
    u = call(merge_kernel, shape((ny_, m // 128, 128), F32), (u,), name="merge")
    u = lax.all_to_all(u, "rows", 0, 0, axis_index_groups=y_groups)
    g = call(last_kernel, shape((m // 128, 128), F32), (u,), name="last")
    return f.reshape(n), g.reshape(m)


def solution(mesh):
    placed = (
        P(None, ("rows", "cols")),
        P(None, ("cols", "rows")),
        P(("rows", "cols")),
        P(("cols", "rows")),
        P("cols"),
    )
    rows, cols = mesh.shape["rows"], mesh.shape["cols"]
    nz = 8
    z_groups = [[a * nz + b for b in range(nz)] for a in range(rows // nz)]
    y_groups = [[a * nz + b for a in range(rows // nz)] for b in range(nz)]
    return jax.shard_map(
        functools.partial(local, (z_groups, y_groups, cols)),
        mesh=mesh,
        in_specs=placed,
        out_specs=(P("rows"), P("cols")),
        check_vma=False,
    )
```

```python
import functools

import jax
import jax.numpy as jnp
from jax import lax
from jax.experimental import pallas as pl
from jax.experimental.pallas import tpu as pltpu
from jax.sharding import Mesh
from jax.sharding import PartitionSpec as P

EPS = 0.05
LOG2E = 1.4426950408889634
LN2 = 0.6931471805599453
BF16 = jnp.bfloat16
F32 = jnp.float32
PIECE = 256
EXTRA = 16
DEPTH = 256
GROUP = 16
LOW = -1e30
VMEM_LIMIT = 56 * 1024 * 1024


def split3(v):
    high = v.astype(BF16).astype(F32)
    rest = v - high
    mid = rest.astype(BF16).astype(F32)
    return high, mid, rest - mid


def wide(ref, row):
    pair = ref[pl.ds(row, 2), :]
    return jnp.concatenate([pair[0:1], pair[1:2]], axis=1)


def put_wide(ref, row, v):
    ref[pl.ds(row, 1), :] = v[:, 0:128]
    ref[pl.ds(row + 1, 1), :] = v[:, 128:256]


def rows_of(terms, count, width):
    row = lax.broadcasted_iota(jnp.int32, (count, width), 0)
    out = jnp.zeros((count, width), F32)
    for index, term in enumerate(terms):
        out = jnp.where(row == index, term, out)
    return out


def pack_kernel(x_ref, y_ref, la_ref, lb_ref, g_ref, xo_ref, yo_ref):
    feat = x_ref.shape[0]
    la = wide(la_ref, 0) * LOG2E
    y = y_ref[...].astype(F32)
    ny = jnp.sum(y * y, axis=0, keepdims=True)
    mine = lax.axis_index("y") * 8 + lax.axis_index("zh") * 2 + lax.axis_index("zl")
    g = wide(g_ref, 2 * mine)
    own = (wide(lb_ref, 0) + (g - ny / feat) / EPS) * LOG2E
    one = jnp.ones((1, PIECE), F32)
    xo_ref[0:feat, :] = x_ref[...]
    xo_ref[feat : feat + EXTRA, :] = rows_of(split3(la), EXTRA, PIECE).astype(BF16)
    yo_ref[0:feat, :] = y_ref[...]
    yo_ref[feat : feat + EXTRA, :] = rows_of(split3(own) + (one, one, one), EXTRA, PIECE).astype(BF16)


def right_side(y_ref, p):
    feat = y_ref.shape[1] - EXTRA
    y = y_ref[p, 0:feat, :]
    extra = y_ref[p, feat : feat + EXTRA, :]
    fill = jnp.zeros((DEPTH - 3 * feat - EXTRA, PIECE), BF16)
    return jnp.concatenate([y, y, y, extra, fill], axis=0)


def dot(a, b):
    return jnp.dot(a, b, preferred_element_type=F32)


IB = 2048
JP = 2


def row_kernel(*refs, scale):
    xs, ys = refs[0:4], refs[4:8]
    out_ref, a_ref, y_ref, nx_ref, la_ref, s_ref, m_ref, l_ref = refs[8:]
    feat = y_ref.shape[1] - EXTRA
    n = GROUP * PIECE
    one = jnp.ones((1, PIECE), F32)
    extra = rows_of((one, one, one), EXTRA, PIECE)
    fill = jnp.zeros((DEPTH - 3 * feat - EXTRA, PIECE), F32)
    xi, zl, core = lax.axis_index("x"), lax.axis_index("zl"), lax.axis_index("c")
    yi, zh = lax.axis_index("y"), lax.axis_index("zh")
    for k in range(4):
        for j in range(4):
            p = ((zl + j // 2) % 2 * 4 + (xi + 4 - k) % 4) * 2 + (core + j % 2) % 2
            x = xs[k][j, 0:feat, :].astype(F32)
            block = jnp.concatenate(split3(x * scale) + (extra, fill), axis=0)
            a_ref[pl.ds(pl.multiple_of(p * PIECE, PIECE), PIECE), :] = jnp.transpose(block).astype(BF16)
            put_wide(nx_ref, 2 * p, jnp.sum(x * x, axis=0, keepdims=True) / feat)
            own = xs[k][j, feat : feat + EXTRA, :].astype(F32)
            put_wide(la_ref, 2 * p, jnp.sum(own, axis=0, keepdims=True))
            y_ref[(yi + 4 - k) % 4 * 4 + (zh + 4 - j) % 4] = ys[k][j]
    m_ref[...] = jnp.full(m_ref.shape, LOW, F32)
    l_ref[...] = jnp.zeros(l_ref.shape, F32)
    blocks = n // IB
    steps = blocks * (GROUP // JP)

    def start(t, k):
        base = pl.multiple_of((t % blocks) * IB, IB)
        return dot(a_ref[pl.ds(base, IB), :], right_side(y_ref, (t // blocks) * JP + k))

    def finish(t, slot, r):
        base = pl.multiple_of((t % blocks) * IB + r, 8)
        rows = pl.ds(base, 8)
        vals = [s_ref[slot, r : r + 8, c * 128 : (c + 1) * 128] for c in range(JP * 2)]
        old = m_ref[rows, :]
        top = old
        for v in vals:
            top = jnp.maximum(top, v)
        acc = l_ref[rows, :] * jnp.exp2(old - top)
        for v in vals:
            acc = acc + jnp.exp2(v - top)
        m_ref[rows, :] = top
        l_ref[rows, :] = acc

    def half(t, slot):
        later = jnp.minimum(t + 1, steps - 1)
        for k in range(JP):
            s_ref[1 - slot, :, k * PIECE : (k + 1) * PIECE] = start(later, k)
            for r in range(k * IB // JP, (k + 1) * IB // JP, 8):
                finish(t, slot, r)

    for k in range(JP):
        s_ref[0, :, k * PIECE : (k + 1) * PIECE] = start(0, k)

    def body(u, carry):
        half(2 * u, 0)
        half(2 * u + 1, 1)
        return carry

    lax.fori_loop(0, steps // 2, body, 0)
    for q in range(n // 128):
        mt = jnp.transpose(m_ref[q * 128 : (q + 1) * 128, :])
        lt = jnp.transpose(l_ref[q * 128 : (q + 1) * 128, :])
        top = jnp.max(mt, axis=0, keepdims=True)
        lse = top + jnp.log2(jnp.sum(lt * jnp.exp2(mt - top), axis=0, keepdims=True))
        for d in range(out_ref.shape[0]):
            out_ref[d, q : q + 1, :] = lse


def col_kernel(a_in, y_ref, nx_ref, la_ref, lse_ref, f_ref, out_ref, a_ref, s_ref, fs_ref):
    feat = y_ref.shape[1] - EXTRA
    n = GROUP * PIECE
    tiles = GROUP
    part = lse_ref[...]
    top = jnp.max(part, axis=0)
    whole = top + jnp.log2(jnp.sum(jnp.exp2(part - top[None]), axis=0))
    fs_ref[...] = nx_ref[...] - (EPS * LN2) * whole
    f_ref[...] = fs_ref[pl.ds(pl.multiple_of(lax.axis_index("zl") * 16, 16), 16), :]
    own = la_ref[...] - whole
    zero = jnp.zeros((1, PIECE), F32)
    keep = 3 * feat - 128
    a_ref[:, 0:128] = a_in[:, 0:128]
    for p in range(GROUP):
        term = jnp.concatenate([own[2 * p : 2 * p + 1], own[2 * p + 1 : 2 * p + 2]], axis=1)
        extra = rows_of((zero, zero, zero) + split3(term), 128 - keep, PIECE)
        rows = slice(p * PIECE, (p + 1) * PIECE)
        a_ref[rows, 128:256] = jnp.concatenate(
            [a_in[rows, 128 : 128 + keep], jnp.transpose(extra).astype(BF16)], axis=1
        )
    chunk = 1024

    def start(t, k):
        return dot(a_ref[k * chunk : (k + 1) * chunk, :], right_side(y_ref, t))

    def fold(s, how):
        return how(s.reshape(s.shape[0] // 8, 8, s.shape[1]), axis=0)

    def half(t, slot, top):
        later = jnp.minimum(t + 1, tiles - 1)
        new = jnp.full((8, PIECE), LOW, F32)
        acc = jnp.zeros((8, PIECE), F32)
        for k in range(n // chunk):
            s = start(later, k)
            s_ref[1 - slot, k * chunk : (k + 1) * chunk, :] = s
            new = jnp.maximum(new, fold(s, jnp.max))
            for r in range(k * chunk, (k + 1) * chunk, 64):
                v = s_ref[slot, r : r + 64, :].reshape(8, 8, PIECE)
                acc = acc + jnp.sum(jnp.exp2(v - top[None]), axis=0)
        peak = jnp.max(top, axis=0, keepdims=True)
        total = jnp.sum(acc * jnp.exp2(top - peak), axis=0, keepdims=True)
        y = y_ref[t, 0:feat, :].astype(F32)
        ny = jnp.sum(y * y, axis=0, keepdims=True)
        u = peak + jnp.log2(total) - ny * (LOG2E / (feat * EPS))
        for d in range(out_ref.shape[0]):
            out_ref[d, pl.ds(2 * t, 1), :] = u[:, 0:128]
            out_ref[d, pl.ds(2 * t + 1, 1), :] = u[:, 128:256]
        return new

    top = jnp.full((8, PIECE), LOW, F32)
    for k in range(n // chunk):
        s = start(0, k)
        s_ref[0, k * chunk : (k + 1) * chunk, :] = s
        top = jnp.maximum(top, fold(s, jnp.max))

    def body(u, top):
        return half(2 * u + 1, 1, half(2 * u, 0, top))

    lax.fori_loop(0, tiles // 2, body, top)


def merge_kernel(u_ref, out_ref):
    u = u_ref[...]
    top = jnp.max(u, axis=0)
    out_ref[...] = (top + jnp.log2(jnp.sum(jnp.exp2(u - top[None]), axis=0))) * (-EPS * LN2)


def last_kernel(mine_ref, other_ref, out_ref):
    first = lax.axis_index("zl") == 0
    mine, other = mine_ref[...], other_ref[...]
    even, odd = jnp.where(first, mine, other), jnp.where(first, other, mine)
    for p in range(GROUP):
        out_ref[4 * p : 4 * p + 2, :] = even[2 * p : 2 * p + 2]
        out_ref[4 * p + 2 : 4 * p + 4, :] = odd[2 * p : 2 * p + 2]


def call(kernel, outs, args, scratch=(), name=None):
    vmem = pl.BlockSpec(memory_space=pltpu.VMEM)
    return pl.pallas_call(
        kernel,
        out_shape=outs,
        in_specs=[vmem] * len(args),
        out_specs=jax.tree.map(lambda _: vmem, outs),
        scratch_shapes=list(scratch),
        compiler_params=pltpu.CompilerParams(vmem_limit_bytes=VMEM_LIMIT),
        name=name,
    )(*args)


def ring(v, axis):
    return [v] + [lax.ppermute(v, axis, [(i, (i + k) % 4) for i in range(4)]) for k in (1, 2, 3)]


def local(x_feat, y_feat, log_a, log_b, g_init):
    feat, piece = x_feat.shape
    scale = 2.0 * LOG2E / (feat * EPS)
    shape = jax.ShapeDtypeStruct
    depth = feat + EXTRA
    n = GROUP * piece
    xo, yo = call(
        pack_kernel,
        [shape((depth, piece), BF16), shape((depth, piece), BF16)],
        (
            x_feat,
            y_feat,
            log_a.reshape(-1, 128),
            log_b.reshape(-1, 128),
            g_init.reshape(-1, 128),
        ),
        name="pack",
    )
    ya = ring(yo, "zh")
    xa = [xo] + [lax.ppermute(xo, ("zl", "c"), [(i, i ^ k) for i in range(4)]) for k in (1, 2, 3)]
    xa, ya = lax.optimization_barrier((xa, ya))
    xb = ring(jnp.stack(xa), "x")
    yb = ring(jnp.stack(ya), "y")
    lse, a, ys, nx, la = call(
        functools.partial(row_kernel, scale=scale),
        [
            shape((GROUP, n // 128, 128), F32),
            shape((n, DEPTH), BF16),
            shape((GROUP, depth, piece), BF16),
            shape((n // 128, 128), F32),
            shape((n // 128, 128), F32),
        ],
        (*xb, *yb),
        [
            pltpu.VMEM((2, IB, JP * PIECE), F32),
            pltpu.VMEM((n, 128), F32),
            pltpu.VMEM((n, 128), F32),
        ],
        name="row_pass",
    )
    parts = lax.all_to_all(lse, ("zl", "x", "c"), 0, 0)
    f, u = call(
        col_kernel,
        [shape((n // 256, 128), F32), shape((GROUP, n // 128, 128), F32)],
        (a, ys, nx, la, parts),
        [
            pltpu.VMEM((n, DEPTH), BF16),
            pltpu.VMEM((2, n, PIECE), F32),
            pltpu.VMEM((n // 128, 128), F32),
        ],
        name="col_pass",
    )
    u = lax.all_to_all(u, ("y", "zh"), 0, 0)
    mine = call(merge_kernel, shape((n // 128, 128), F32), (u,), name="merge")
    other = lax.ppermute(mine, "zl", [(0, 1), (1, 0)])
    g = call(last_kernel, shape((n // 64, 128), F32), (mine, other), name="last")
    return f.reshape(n // 2), g.reshape(2 * n)


def solution(mesh):
    inner = Mesh(mesh.devices.reshape(4, 4, 2, 4, 2), ("y", "zh", "zl", "x", "c"))
    rows, cols = ("y", "zh", "zl"), ("x", "c")
    placed = (P(None, rows + cols), P(None, cols + rows), P(rows + cols), P(cols + rows), P(cols))
    return jax.shard_map(
        local, mesh=inner, in_specs=placed, out_specs=(P(rows), P(cols)), check_vma=False
    )
```

```python
import functools

import jax
import jax.numpy as jnp
from jax import lax
from jax.experimental import pallas as pl
from jax.experimental.pallas import tpu as pltpu
from jax.sharding import Mesh
from jax.sharding import PartitionSpec as P

EPS = 0.05
LOG2E = 1.4426950408889634
LN2 = 0.6931471805599453
BF16 = jnp.bfloat16
F32 = jnp.float32
PIECE = 256
EXTRA = 16
DEPTH = 256
GROUP = 16
LOW = -1e30
VMEM_LIMIT = 24 * 1024 * 1024


def split3(v):
    high = v.astype(BF16).astype(F32)
    rest = v - high
    mid = rest.astype(BF16).astype(F32)
    return high, mid, rest - mid


def wide(ref, row):
    pair = ref[pl.ds(row, 2), :]
    return jnp.concatenate([pair[0:1], pair[1:2]], axis=1)


def put_wide(ref, row, v):
    ref[pl.ds(row, 1), :] = v[:, 0:128]
    ref[pl.ds(row + 1, 1), :] = v[:, 128:256]


def rows_of(terms, count, width):
    row = lax.broadcasted_iota(jnp.int32, (count, width), 0)
    out = jnp.zeros((count, width), F32)
    for index, term in enumerate(terms):
        out = jnp.where(row == index, term, out)
    return out


def pack_kernel(x_ref, y_ref, la_ref, lb_ref, g_ref, xo_ref, yo_ref):
    feat = x_ref.shape[0]
    la = wide(la_ref, 0) * LOG2E
    y = y_ref[...].astype(F32)
    ny = jnp.sum(y * y, axis=0, keepdims=True)
    mine = lax.axis_index("y") * 8 + lax.axis_index("zh") * 2 + lax.axis_index("zl")
    g = wide(g_ref, 2 * mine)
    own = (wide(lb_ref, 0) + (g - ny / feat) / EPS) * LOG2E
    one = jnp.ones((1, PIECE), F32)
    xo_ref[0:feat, :] = x_ref[...]
    xo_ref[feat : feat + EXTRA, :] = rows_of(split3(la) + (one, one, one), EXTRA, PIECE).astype(BF16)
    yo_ref[0:feat, :] = y_ref[...]
    yo_ref[feat : feat + EXTRA, :] = rows_of(split3(own) + (one, one, one), EXTRA, PIECE).astype(BF16)


def left_side(ref, scale, term):
    feat = ref.shape[0] - EXTRA
    zero = jnp.zeros((1, PIECE), F32)
    extra = rows_of((zero, zero, zero) + split3(term), DEPTH - 3 * feat, PIECE)
    parts = split3(ref[0:feat, :].astype(F32) * scale)
    return jnp.transpose(jnp.concatenate(parts + (extra,), axis=0)).astype(BF16)


def right_side(ref, p):
    feat = ref.shape[1] - EXTRA
    v = ref[p, 0:feat, :]
    extra = ref[p, feat : feat + EXTRA, :]
    fill = jnp.zeros((DEPTH - 3 * feat - EXTRA, PIECE), BF16)
    return jnp.concatenate([v, v, v, extra, fill], axis=0)


def own_term(ref):
    feat = ref.shape[0] - EXTRA
    row = lax.broadcasted_iota(jnp.int32, (EXTRA, PIECE), 0)
    extra = ref[feat : feat + EXTRA, :].astype(F32)
    return jnp.sum(jnp.where(row < 3, extra, 0.0), axis=0, keepdims=True)


def norm(ref):
    feat = ref.shape[0] - EXTRA
    v = ref[0:feat, :].astype(F32)
    return jnp.sum(v * v, axis=0, keepdims=True)


def fold(s, how):
    return how(s.reshape(s.shape[0] // 8, 8, s.shape[1]), axis=0)


CHUNK = 1024
SAMPLE = 256
ROOM = 100.0


def sweep(a_ref, r_ref, top_ref, peak_ref, acc_ref):
    n, tiles = a_ref.shape[0], r_ref.shape[0]

    def dot(first, count, right):
        return jnp.dot(a_ref[first : first + count, :], right, preferred_element_type=F32)

    def sample(t):
        return jnp.max(dot(0, SAMPLE, right_side(r_ref, t)), axis=0, keepdims=True)

    def total(t, top, peak):
        right = right_side(r_ref, t)
        acc = jnp.zeros((8, PIECE), F32)
        for first in range(0, n, CHUNK):
            s = dot(first, CHUNK, right)
            if peak is not None:
                peak = jnp.maximum(peak, fold(s, jnp.max))
            acc = acc + fold(jnp.exp2(s - top), jnp.sum)
        top_ref[t] = jnp.broadcast_to(top, (8, PIECE))
        acc_ref[t] = acc
        return peak

    def body(u, top):
        for t in (2 * u, 2 * u + 1):
            peak_ref[t] = total(t, top, jnp.full((8, PIECE), LOW, F32))
            top = sample(jnp.minimum(t + 1, tiles - 1))
        return top

    lax.fori_loop(0, tiles // 2, body, sample(0))

    @pl.when(jnp.max(peak_ref[...] - top_ref[...]) > ROOM)
    def _():
        def again(t, carry):
            @pl.when(jnp.max(peak_ref[t] - top_ref[t]) > ROOM)
            def _():
                total(t, jnp.max(peak_ref[t], axis=0, keepdims=True), None)

            return carry

        lax.fori_loop(0, tiles, again, 0)


def lse_of(top_ref, acc_ref, t):
    return top_ref[t, 0:1, :] + jnp.log2(jnp.sum(acc_ref[t], axis=0, keepdims=True))


def row_kernel(*refs, scale):
    xs, ys = refs[0:4], refs[4:8]
    out_ref, x_ref, y_ref, a_ref, top_ref, peak_ref, acc_ref = refs[8:]
    xi, zl, core = lax.axis_index("x"), lax.axis_index("zl"), lax.axis_index("c")
    yi, zh = lax.axis_index("y"), lax.axis_index("zh")
    for k in range(4):
        for j in range(4):
            x_ref[((zl + j // 2) % 2 * 4 + (xi + 4 - k) % 4) * 2 + (core + j % 2) % 2] = xs[k][j]
            y_ref[(yi + 4 - k) % 4 * 4 + (zh + 4 - j) % 4] = ys[k][j]
            p = 4 * k + j
            left = left_side(ys[k].at[j], scale, own_term(ys[k].at[j]))
            a_ref[p * PIECE : (p + 1) * PIECE, :] = left
    sweep(a_ref, x_ref, top_ref, peak_ref, acc_ref)
    for p in range(GROUP):
        lse = lse_of(top_ref, acc_ref, p)
        for d in range(out_ref.shape[0]):
            put_wide(out_ref.at[d], 2 * p, lse)


def col_kernel(x_ref, y_ref, lse_ref, f_ref, out_ref, a_ref, top_ref, peak_ref, acc_ref, fs_ref, *, scale):
    feat = x_ref.shape[1] - EXTRA
    part = lse_ref[...]
    top = jnp.max(part, axis=0)
    whole = top + jnp.log2(jnp.sum(jnp.exp2(part - top[None]), axis=0))
    for p in range(GROUP):
        lse = jnp.concatenate([whole[2 * p : 2 * p + 1], whole[2 * p + 1 : 2 * p + 2]], axis=1)
        put_wide(fs_ref, 2 * p, norm(x_ref.at[p]) / feat - (EPS * LN2) * lse)
        left = left_side(x_ref.at[p], scale, own_term(x_ref.at[p]) - lse)
        a_ref[p * PIECE : (p + 1) * PIECE, :] = left
    f_ref[...] = fs_ref[pl.ds(pl.multiple_of(lax.axis_index("zl") * GROUP, GROUP), GROUP), :]
    sweep(a_ref, y_ref, top_ref, peak_ref, acc_ref)
    for p in range(GROUP):
        u = lse_of(top_ref, acc_ref, p) - norm(y_ref.at[p]) * (LOG2E / (feat * EPS))
        for d in range(out_ref.shape[0]):
            put_wide(out_ref.at[d], 2 * p, u)


def merge_kernel(u_ref, out_ref):
    u = u_ref[...]
    top = jnp.max(u, axis=0)
    out_ref[...] = (top + jnp.log2(jnp.sum(jnp.exp2(u - top[None]), axis=0))) * (-EPS * LN2)


def last_kernel(mine_ref, other_ref, out_ref):
    first = lax.axis_index("zl") == 0
    mine, other = mine_ref[...], other_ref[...]
    even, odd = jnp.where(first, mine, other), jnp.where(first, other, mine)
    for p in range(GROUP):
        out_ref[4 * p : 4 * p + 2, :] = even[2 * p : 2 * p + 2]
        out_ref[4 * p + 2 : 4 * p + 4, :] = odd[2 * p : 2 * p + 2]


def call(kernel, outs, args, scratch=(), name=None):
    vmem = pl.BlockSpec(memory_space=pltpu.VMEM)
    return pl.pallas_call(
        kernel,
        out_shape=outs,
        in_specs=[vmem] * len(args),
        out_specs=jax.tree.map(lambda _: vmem, outs),
        scratch_shapes=list(scratch),
        compiler_params=pltpu.CompilerParams(vmem_limit_bytes=VMEM_LIMIT),
        name=name,
    )(*args)


def ring(v, axis):
    return [v] + [lax.ppermute(v, axis, [(i, (i + k) % 4) for i in range(4)]) for k in (1, 2, 3)]


def local(x_feat, y_feat, log_a, log_b, g_init):
    feat, piece = x_feat.shape
    scale = 2.0 * LOG2E / (feat * EPS)
    shape = jax.ShapeDtypeStruct
    depth = feat + EXTRA
    n = GROUP * piece
    xo, yo = call(
        pack_kernel,
        [shape((depth, piece), BF16), shape((depth, piece), BF16)],
        (
            x_feat,
            y_feat,
            log_a.reshape(-1, 128),
            log_b.reshape(-1, 128),
            g_init.reshape(-1, 128),
        ),
        name="pack",
    )
    ya = ring(yo, "zh")
    xa = [xo] + [lax.ppermute(xo, ("zl", "c"), [(i, i ^ k) for i in range(4)]) for k in (1, 2, 3)]
    xa, ya = lax.optimization_barrier((xa, ya))
    xb = ring(jnp.stack(xa), "x")
    yb = ring(jnp.stack(ya), "y")
    left = pltpu.VMEM((n, DEPTH), BF16)
    stats = [pltpu.VMEM((GROUP, 8, piece), F32)] * 3
    pieces = shape((GROUP, depth, piece), BF16)
    spread = shape((GROUP, n // 128, 128), F32)
    lse, xs, ys = call(
        functools.partial(row_kernel, scale=scale),
        [spread, pieces, pieces],
        (*xb, *yb),
        [left] + stats,
        name="row_pass",
    )
    parts = lax.all_to_all(lse, ("zl", "x", "c"), 0, 0)
    f, u = call(
        functools.partial(col_kernel, scale=scale),
        [shape((n // 256, 128), F32), spread],
        (xs, ys, parts),
        [left] + stats + [pltpu.VMEM((n // 128, 128), F32)],
        name="col_pass",
    )
    u = lax.all_to_all(u, ("y", "zh"), 0, 0)
    mine = call(merge_kernel, shape((n // 128, 128), F32), (u,), name="merge")
    other = lax.ppermute(mine, "zl", [(0, 1), (1, 0)])
    g = call(last_kernel, shape((n // 64, 128), F32), (mine, other), name="last")
    return f.reshape(n // 2), g.reshape(2 * n)


def solution(mesh):
    inner = Mesh(mesh.devices.reshape(4, 4, 2, 4, 2), ("y", "zh", "zl", "x", "c"))
    rows, cols = ("y", "zh", "zl"), ("x", "c")
    placed = (P(None, rows + cols), P(None, cols + rows), P(rows + cols), P(cols + rows), P(cols))
    return jax.shard_map(
        local, mesh=inner, in_specs=placed, out_specs=(P(rows), P(cols)), check_vma=False
    )
```

```python
import functools

import jax
import jax.numpy as jnp
from jax import lax
from jax.experimental import pallas as pl
from jax.experimental.pallas import tpu as pltpu
from jax.sharding import Mesh
from jax.sharding import PartitionSpec as P

EPS = 0.05
LOG2E = 1.4426950408889634
LN2 = 0.6931471805599453
BF16 = jnp.bfloat16
F32 = jnp.float32
PIECE = 256
EXTRA = 16
DEPTH = 256
GROUP = 16
LOW = -1e30
VMEM_LIMIT = 24 * 1024 * 1024


def split3(v):
    high = v.astype(BF16).astype(F32)
    rest = v - high
    mid = rest.astype(BF16).astype(F32)
    return high, mid, rest - mid


def wide(ref, row):
    pair = ref[pl.ds(row, 2), :]
    return jnp.concatenate([pair[0:1], pair[1:2]], axis=1)


def put_wide(ref, row, v):
    ref[pl.ds(row, 1), :] = v[:, 0:128]
    ref[pl.ds(row + 1, 1), :] = v[:, 128:256]


def rows_of(terms, count, width):
    row = lax.broadcasted_iota(jnp.int32, (count, width), 0)
    out = jnp.zeros((count, width), F32)
    for index, term in enumerate(terms):
        out = jnp.where(row == index, term, out)
    return out


def pack_kernel(x_ref, y_ref, la_ref, lb_ref, g_ref, xo_ref, yo_ref):
    feat = x_ref.shape[0]
    la = wide(la_ref, 0) * LOG2E
    y = y_ref[...].astype(F32)
    ny = jnp.sum(y * y, axis=0, keepdims=True)
    mine = lax.axis_index("y") * 8 + lax.axis_index("zh") * 2 + lax.axis_index("zl")
    g = wide(g_ref, 2 * mine)
    own = (wide(lb_ref, 0) + (g - ny / feat) / EPS) * LOG2E
    one = jnp.ones((1, PIECE), F32)
    xo_ref[0:feat, :] = x_ref[...]
    xo_ref[feat : feat + EXTRA, :] = rows_of(split3(la) + (one, one, one), EXTRA, PIECE).astype(BF16)
    yo_ref[0:feat, :] = y_ref[...]
    yo_ref[feat : feat + EXTRA, :] = rows_of(split3(own) + (one, one, one), EXTRA, PIECE).astype(BF16)


def left_side(ref, scale, term):
    feat = ref.shape[0] - EXTRA
    zero = jnp.zeros((1, PIECE), F32)
    extra = rows_of((zero, zero, zero) + split3(term), DEPTH - 3 * feat, PIECE)
    parts = split3(ref[0:feat, :].astype(F32) * scale)
    return jnp.transpose(jnp.concatenate(parts + (extra,), axis=0)).astype(BF16)


def right_side(ref, p):
    feat = ref.shape[1] - EXTRA
    v = ref[p, 0:feat, :]
    extra = ref[p, feat : feat + EXTRA, :]
    fill = jnp.zeros((DEPTH - 3 * feat - EXTRA, PIECE), BF16)
    return jnp.concatenate([v, v, v, extra, fill], axis=0)


def own_term(ref):
    feat = ref.shape[0] - EXTRA
    row = lax.broadcasted_iota(jnp.int32, (EXTRA, PIECE), 0)
    extra = ref[feat : feat + EXTRA, :].astype(F32)
    return jnp.sum(jnp.where(row < 3, extra, 0.0), axis=0, keepdims=True)


def norm(ref):
    feat = ref.shape[0] - EXTRA
    v = ref[0:feat, :].astype(F32)
    return jnp.sum(v * v, axis=0, keepdims=True)


def fold(s, how):
    return how(s.reshape(s.shape[0] // 8, 8, s.shape[1]), axis=0)


CHUNK = 1024
SAMPLE = 64
LIFT = 60.0
ROOM = 100.0


def sweep(a_ref, r_ref, top_ref, peak_ref, acc_ref):
    n, tiles = a_ref.shape[0], r_ref.shape[0]

    def dot(first, count, right):
        return jnp.dot(a_ref[first : first + count, :], right, preferred_element_type=F32)

    def sample(t):
        return jnp.max(dot(0, SAMPLE, right_side(r_ref, t)), axis=0, keepdims=True) + LIFT

    def total(t, top, peak):
        right = right_side(r_ref, t)
        acc = jnp.zeros((8, PIECE), F32)
        for first in range(0, n, CHUNK):
            s = dot(first, CHUNK, right)
            if peak is not None:
                peak = jnp.maximum(peak, fold(s, jnp.max))
            acc = acc + fold(jnp.exp2(s - top), jnp.sum)
        top_ref[t] = jnp.broadcast_to(top, (8, PIECE))
        acc_ref[t] = acc
        return peak

    def body(u, top):
        for t in (4 * u, 4 * u + 1, 4 * u + 2, 4 * u + 3):
            later = sample(jnp.minimum(t + 1, tiles - 1))
            peak_ref[t] = total(t, top, jnp.full((8, PIECE), LOW, F32))
            top = later
        return top

    lax.fori_loop(0, tiles // 4, body, sample(0))

    over = jnp.max(jnp.max(peak_ref[...] - top_ref[...], axis=1), axis=1, keepdims=True) > ROOM
    bits = jnp.exp2(lax.broadcasted_iota(jnp.int32, (tiles, 1), 0).astype(F32))
    mask = jnp.sum(jnp.where(over, bits, 0.0)).astype(jnp.int32)

    @pl.when(mask > 0)
    def _():
        def again(t, carry):
            @pl.when((mask >> t) & 1 == 1)
            def _():
                total(t, jnp.max(peak_ref[t], axis=0, keepdims=True), None)

            return carry

        lax.fori_loop(0, tiles, again, 0)


def lse_of(top_ref, acc_ref, t):
    return top_ref[t, 0:1, :] + jnp.log2(jnp.sum(acc_ref[t], axis=0, keepdims=True))


def row_kernel(*refs, scale):
    xs, ys = refs[0:4], refs[4:8]
    out_ref, x_ref, y_ref, a_ref, top_ref, peak_ref, acc_ref = refs[8:]
    xi, zl, core = lax.axis_index("x"), lax.axis_index("zl"), lax.axis_index("c")
    yi, zh = lax.axis_index("y"), lax.axis_index("zh")
    for k in range(4):
        for j in range(4):
            x_ref[((zl + j // 2) % 2 * 4 + (xi + 4 - k) % 4) * 2 + (core + j % 2) % 2] = xs[k][j]
            y_ref[(yi + 4 - k) % 4 * 4 + (zh + 4 - j) % 4] = ys[k][j]
            p = 4 * k + j
            left = left_side(ys[k].at[j], scale, own_term(ys[k].at[j]))
            a_ref[p * PIECE : (p + 1) * PIECE, :] = left
    sweep(a_ref, x_ref, top_ref, peak_ref, acc_ref)
    for p in range(GROUP):
        lse = lse_of(top_ref, acc_ref, p)
        for d in range(out_ref.shape[0]):
            put_wide(out_ref.at[d], 2 * p, lse)


def col_kernel(x_ref, y_ref, lse_ref, f_ref, out_ref, a_ref, top_ref, peak_ref, acc_ref, fs_ref, *, scale):
    feat = x_ref.shape[1] - EXTRA
    part = lse_ref[...]
    top = jnp.max(part, axis=0)
    whole = top + jnp.log2(jnp.sum(jnp.exp2(part - top[None]), axis=0))
    for p in range(GROUP):
        lse = jnp.concatenate([whole[2 * p : 2 * p + 1], whole[2 * p + 1 : 2 * p + 2]], axis=1)
        put_wide(fs_ref, 2 * p, norm(x_ref.at[p]) / feat - (EPS * LN2) * lse)
        left = left_side(x_ref.at[p], scale, own_term(x_ref.at[p]) - lse)
        a_ref[p * PIECE : (p + 1) * PIECE, :] = left
    f_ref[...] = fs_ref[pl.ds(pl.multiple_of(lax.axis_index("zl") * GROUP, GROUP), GROUP), :]
    sweep(a_ref, y_ref, top_ref, peak_ref, acc_ref)
    for p in range(GROUP):
        u = lse_of(top_ref, acc_ref, p) - norm(y_ref.at[p]) * (LOG2E / (feat * EPS))
        for d in range(out_ref.shape[0]):
            put_wide(out_ref.at[d], 2 * p, u)


def merge_kernel(u_ref, out_ref):
    u = u_ref[...]
    top = jnp.max(u, axis=0)
    out_ref[...] = (top + jnp.log2(jnp.sum(jnp.exp2(u - top[None]), axis=0))) * (-EPS * LN2)


def last_kernel(mine_ref, other_ref, out_ref):
    first = lax.axis_index("zl") == 0
    mine, other = mine_ref[...], other_ref[...]
    even, odd = jnp.where(first, mine, other), jnp.where(first, other, mine)
    for p in range(GROUP):
        out_ref[4 * p : 4 * p + 2, :] = even[2 * p : 2 * p + 2]
        out_ref[4 * p + 2 : 4 * p + 4, :] = odd[2 * p : 2 * p + 2]


def call(kernel, outs, args, scratch=(), name=None, vmem_limit=VMEM_LIMIT):
    vmem = pl.BlockSpec(memory_space=pltpu.VMEM)
    return pl.pallas_call(
        kernel,
        out_shape=outs,
        in_specs=[vmem] * len(args),
        out_specs=jax.tree.map(lambda _: vmem, outs),
        scratch_shapes=list(scratch),
        compiler_params=pltpu.CompilerParams(vmem_limit_bytes=vmem_limit),
        name=name,
    )(*args)


def ring(v, axis):
    return [v] + [lax.ppermute(v, axis, [(i, (i + k) % 4) for i in range(4)]) for k in (1, 2, 3)]


def local(x_feat, y_feat, log_a, log_b, g_init):
    feat, piece = x_feat.shape
    scale = 2.0 * LOG2E / (feat * EPS)
    shape = jax.ShapeDtypeStruct
    depth = feat + EXTRA
    n = GROUP * piece
    xo, yo = call(
        pack_kernel,
        [shape((depth, piece), BF16), shape((depth, piece), BF16)],
        (
            x_feat,
            y_feat,
            log_a.reshape(-1, 128),
            log_b.reshape(-1, 128),
            g_init.reshape(-1, 128),
        ),
        name="pack",
        vmem_limit=60 * 1024 * 1024,
    )
    ya = ring(yo, "zh")
    xa = [xo] + [lax.ppermute(xo, ("zl", "c"), [(i, i ^ k) for i in range(4)]) for k in (1, 2, 3)]
    xa, ya = lax.optimization_barrier((xa, ya))
    xb = ring(jnp.stack(xa), "x")
    yb = ring(jnp.stack(ya), "y")
    left = pltpu.VMEM((n, DEPTH), BF16)
    stats = [pltpu.VMEM((GROUP, 8, piece), F32)] * 3
    pieces = shape((GROUP, depth, piece), BF16)
    spread = shape((GROUP, n // 128, 128), F32)
    lse, xs, ys = call(
        functools.partial(row_kernel, scale=scale),
        [spread, pieces, pieces],
        (*xb, *yb),
        [left] + stats,
        name="row_pass",
    )
    parts = lax.all_to_all(lse, ("zl", "x", "c"), 0, 0)
    f, u = call(
        functools.partial(col_kernel, scale=scale),
        [shape((n // 256, 128), F32), spread],
        (xs, ys, parts),
        [left] + stats + [pltpu.VMEM((n // 128, 128), F32)],
        name="col_pass",
    )
    u = lax.all_to_all(u, ("y", "zh"), 0, 0)
    mine = call(merge_kernel, shape((n // 128, 128), F32), (u,), name="merge")
    other = lax.ppermute(mine, "zl", [(0, 1), (1, 0)])
    g = call(last_kernel, shape((n // 64, 128), F32), (mine, other), name="last")
    return f.reshape(n // 2), g.reshape(2 * n)


def solution(mesh):
    inner = Mesh(mesh.devices.reshape(4, 4, 2, 4, 2), ("y", "zh", "zl", "x", "c"))
    rows, cols = ("y", "zh", "zl"), ("x", "c")
    placed = (P(None, rows + cols), P(None, cols + rows), P(rows + cols), P(cols + rows), P(cols))
    return jax.shard_map(
        local, mesh=inner, in_specs=placed, out_specs=(P(rows), P(cols)), check_vma=False
    )
```

```python
import functools

import jax
import jax.numpy as jnp
from jax import lax
from jax.experimental import pallas as pl
from jax.experimental.pallas import tpu as pltpu
from jax.sharding import Mesh
from jax.sharding import PartitionSpec as P

EPS = 0.05
LOG2E = 1.4426950408889634
LN2 = 0.6931471805599453
BF16 = jnp.bfloat16
F32 = jnp.float32
PIECE = 256
EXTRA = 16
DEPTH = 256
GROUP = 16
LOW = -1e30
VMEM_LIMIT = 24 * 1024 * 1024


def split3(v):
    high = v.astype(BF16).astype(F32)
    rest = v - high
    mid = rest.astype(BF16).astype(F32)
    return high, mid, rest - mid


def wide(ref, row):
    pair = ref[pl.ds(row, 2), :]
    return jnp.concatenate([pair[0:1], pair[1:2]], axis=1)


def put_wide(ref, row, v):
    ref[pl.ds(row, 1), :] = v[:, 0:128]
    ref[pl.ds(row + 1, 1), :] = v[:, 128:256]


def rows_of(terms, count, width):
    row = lax.broadcasted_iota(jnp.int32, (count, width), 0)
    out = jnp.zeros((count, width), F32)
    for index, term in enumerate(terms):
        out = jnp.where(row == index, term, out)
    return out


def pack_kernel(x_ref, y_ref, la_ref, lb_ref, g_ref, xo_ref, yo_ref):
    feat = x_ref.shape[0]
    la = wide(la_ref, 0) * LOG2E
    y = y_ref[...].astype(F32)
    ny = jnp.sum(y * y, axis=0, keepdims=True)
    mine = lax.axis_index("y") * 8 + lax.axis_index("zh") * 2 + lax.axis_index("zl")
    g = wide(g_ref, 2 * mine)
    own = (wide(lb_ref, 0) + (g - ny / feat) / EPS) * LOG2E
    one = jnp.ones((1, PIECE), F32)
    xo_ref[0:feat, :] = x_ref[...]
    xo_ref[feat : feat + EXTRA, :] = rows_of(split3(la) + (one, one, one), EXTRA, PIECE).astype(BF16)
    yo_ref[0:feat, :] = y_ref[...]
    yo_ref[feat : feat + EXTRA, :] = rows_of(split3(own) + (one, one, one), EXTRA, PIECE).astype(BF16)


def left_side(ref, scale, term):
    feat = ref.shape[0] - EXTRA
    zero = jnp.zeros((1, PIECE), F32)
    extra = rows_of((zero, zero, zero) + split3(term), DEPTH - 3 * feat, PIECE)
    parts = split3(ref[0:feat, :].astype(F32) * scale)
    return jnp.transpose(jnp.concatenate(parts + (extra,), axis=0)).astype(BF16)


def right_side(ref, p):
    feat = ref.shape[1] - EXTRA
    v = ref[p, 0:feat, :]
    extra = ref[p, feat : feat + EXTRA, :]
    fill = jnp.zeros((DEPTH - 3 * feat - EXTRA, PIECE), BF16)
    return jnp.concatenate([v, v, v, extra, fill], axis=0)


def own_term(ref):
    feat = ref.shape[0] - EXTRA
    row = lax.broadcasted_iota(jnp.int32, (EXTRA, PIECE), 0)
    extra = ref[feat : feat + EXTRA, :].astype(F32)
    return jnp.sum(jnp.where(row < 3, extra, 0.0), axis=0, keepdims=True)


def norm(ref):
    feat = ref.shape[0] - EXTRA
    v = ref[0:feat, :].astype(F32)
    return jnp.sum(v * v, axis=0, keepdims=True)


def fold(s, how):
    return how(s.reshape(s.shape[0] // 8, 8, s.shape[1]), axis=0)


CHUNK = 1024
SAMPLE = 64
LIFT = 60.0
ROOM = 100.0


def sweep(a_ref, r_ref, top_ref, peak_ref, acc_ref):
    n, tiles = a_ref.shape[0], r_ref.shape[0]

    def dot(first, count, right):
        return jnp.dot(a_ref[first : first + count, :], right, preferred_element_type=F32)

    def sample(t):
        return jnp.max(dot(0, SAMPLE, right_side(r_ref, t)), axis=0, keepdims=True) + LIFT

    def total(t, top, peak):
        right = right_side(r_ref, t)
        acc = jnp.zeros((8, PIECE), F32)
        for first in range(0, n, CHUNK):
            s = dot(first, CHUNK, right)
            if peak is not None:
                peak = jnp.maximum(peak, fold(s, jnp.max))
            acc = acc + fold(jnp.exp2(s - top), jnp.sum)
        top_ref[t] = jnp.broadcast_to(top, (8, PIECE))
        acc_ref[t] = acc
        return peak

    def body(u, top):
        for t in (4 * u, 4 * u + 1, 4 * u + 2, 4 * u + 3):
            later = sample(jnp.minimum(t + 1, tiles - 1))
            peak_ref[t] = total(t, top, jnp.full((8, PIECE), LOW, F32))
            top = later
        return top

    lax.fori_loop(0, tiles // 4, body, sample(0))

    over = jnp.max(jnp.max(peak_ref[...] - top_ref[...], axis=1), axis=1, keepdims=True) > ROOM
    bits = jnp.exp2(lax.broadcasted_iota(jnp.int32, (tiles, 1), 0).astype(F32))
    mask = jnp.sum(jnp.where(over, bits, 0.0)).astype(jnp.int32)

    @pl.when(mask > 0)
    def _():
        def again(t, carry):
            @pl.when((mask >> t) & 1 == 1)
            def _():
                total(t, jnp.max(peak_ref[t], axis=0, keepdims=True), None)

            return carry

        lax.fori_loop(0, tiles, again, 0)


def lse_of(top_ref, acc_ref, t):
    return top_ref[t, 0:1, :] + jnp.log2(jnp.sum(acc_ref[t], axis=0, keepdims=True))


def row_kernel(*refs, scale):
    xs, ys = refs[0:4], refs[4:8]
    out_ref, x_ref, y_ref, a_ref, top_ref, peak_ref, acc_ref = refs[8:]
    xi, zl, core = lax.axis_index("x"), lax.axis_index("zl"), lax.axis_index("c")
    yi, zh = lax.axis_index("y"), lax.axis_index("zh")
    for k in range(4):
        for j in range(4):
            x_ref[((zl + k // 2) % 2 * 4 + (xi + 4 - j) % 4) * 2 + (core + k % 2) % 2] = xs[k][j]
            y_ref[(yi + 4 - k) % 4 * 4 + (zh + 4 - j) % 4] = ys[k][j]
            p = 4 * k + j
            left = left_side(ys[k].at[j], scale, own_term(ys[k].at[j]))
            a_ref[p * PIECE : (p + 1) * PIECE, :] = left
    sweep(a_ref, x_ref, top_ref, peak_ref, acc_ref)
    for p in range(GROUP):
        lse = lse_of(top_ref, acc_ref, p)
        for d in range(out_ref.shape[0]):
            put_wide(out_ref.at[d], 2 * p, lse)


def col_kernel(x_ref, y_ref, lse_ref, f_ref, out_ref, a_ref, top_ref, peak_ref, acc_ref, fs_ref, *, scale):
    feat = x_ref.shape[1] - EXTRA
    part = lse_ref[...]
    top = jnp.max(part, axis=0)
    whole = top + jnp.log2(jnp.sum(jnp.exp2(part - top[None]), axis=0))
    for p in range(GROUP):
        lse = jnp.concatenate([whole[2 * p : 2 * p + 1], whole[2 * p + 1 : 2 * p + 2]], axis=1)
        put_wide(fs_ref, 2 * p, norm(x_ref.at[p]) / feat - (EPS * LN2) * lse)
        left = left_side(x_ref.at[p], scale, own_term(x_ref.at[p]) - lse)
        a_ref[p * PIECE : (p + 1) * PIECE, :] = left
    f_ref[...] = fs_ref[pl.ds(pl.multiple_of(lax.axis_index("zl") * GROUP, GROUP), GROUP), :]
    sweep(a_ref, y_ref, top_ref, peak_ref, acc_ref)
    for p in range(GROUP):
        u = lse_of(top_ref, acc_ref, p) - norm(y_ref.at[p]) * (LOG2E / (feat * EPS))
        for d in range(out_ref.shape[0]):
            put_wide(out_ref.at[d], 2 * p, u)


def merge_kernel(u_ref, out_ref):
    u = u_ref[...]
    top = jnp.max(u, axis=0)
    out_ref[...] = (top + jnp.log2(jnp.sum(jnp.exp2(u - top[None]), axis=0))) * (-EPS * LN2)


def last_kernel(mine_ref, other_ref, out_ref):
    first = lax.axis_index("zl") == 0
    mine, other = mine_ref[...], other_ref[...]
    even, odd = jnp.where(first, mine, other), jnp.where(first, other, mine)
    for p in range(GROUP):
        out_ref[4 * p : 4 * p + 2, :] = even[2 * p : 2 * p + 2]
        out_ref[4 * p + 2 : 4 * p + 4, :] = odd[2 * p : 2 * p + 2]


def call(kernel, outs, args, scratch=(), name=None, vmem_limit=VMEM_LIMIT):
    vmem = pl.BlockSpec(memory_space=pltpu.VMEM)
    return pl.pallas_call(
        kernel,
        out_shape=outs,
        in_specs=[vmem] * len(args),
        out_specs=jax.tree.map(lambda _: vmem, outs),
        scratch_shapes=list(scratch),
        compiler_params=pltpu.CompilerParams(vmem_limit_bytes=vmem_limit),
        name=name,
    )(*args)


def ring(v, axis):
    return [v] + [lax.ppermute(v, axis, [(i, (i + k) % 4) for i in range(4)]) for k in (1, 2, 3)]


def local(x_feat, y_feat, log_a, log_b, g_init):
    feat, piece = x_feat.shape
    scale = 2.0 * LOG2E / (feat * EPS)
    shape = jax.ShapeDtypeStruct
    depth = feat + EXTRA
    n = GROUP * piece
    xo, yo = call(
        pack_kernel,
        [shape((depth, piece), BF16), shape((depth, piece), BF16)],
        (
            x_feat,
            y_feat,
            log_a.reshape(-1, 128),
            log_b.reshape(-1, 128),
            g_init.reshape(-1, 128),
        ),
        name="pack",
        vmem_limit=60 * 1024 * 1024,
    )
    ya = ring(yo, "zh")
    xa = ring(xo, "x")
    ya, xa = lax.optimization_barrier((ya, xa))
    yb = ring(jnp.stack(ya), "y")
    pair = [(0, 1), (1, 0)]
    xb = [jnp.stack(xa)]
    xb.append(lax.ppermute(xb[0], "c", pair))
    xb.append(lax.ppermute(xb[0], "zl", pair))
    xb.append(lax.ppermute(xb[2], "c", pair))
    left = pltpu.VMEM((n, DEPTH), BF16)
    stats = [pltpu.VMEM((GROUP, 8, piece), F32)] * 3
    pieces = shape((GROUP, depth, piece), BF16)
    spread = shape((GROUP, n // 128, 128), F32)
    lse, xs, ys = call(
        functools.partial(row_kernel, scale=scale),
        [spread, pieces, pieces],
        (*xb, *yb),
        [left] + stats,
        name="row_pass",
    )
    parts = lax.all_to_all(lse, ("zl", "x", "c"), 0, 0)
    f, u = call(
        functools.partial(col_kernel, scale=scale),
        [shape((n // 256, 128), F32), spread],
        (xs, ys, parts),
        [left] + stats + [pltpu.VMEM((n // 128, 128), F32)],
        name="col_pass",
    )
    u = lax.all_to_all(u, ("y", "zh"), 0, 0)
    mine = call(merge_kernel, shape((n // 128, 128), F32), (u,), name="merge")
    other = lax.ppermute(mine, "zl", [(0, 1), (1, 0)])
    g = call(last_kernel, shape((n // 64, 128), F32), (mine, other), name="last")
    return f.reshape(n // 2), g.reshape(2 * n)


def solution(mesh):
    inner = Mesh(mesh.devices.reshape(4, 4, 2, 4, 2), ("y", "zh", "zl", "x", "c"))
    rows, cols = ("y", "zh", "zl"), ("x", "c")
    placed = (P(None, rows + cols), P(None, cols + rows), P(rows + cols), P(cols + rows), P(cols))
    return jax.shard_map(
        local, mesh=inner, in_specs=placed, out_specs=(P(rows), P(cols)), check_vma=False
    )
```

```python
import functools

import jax
import jax.numpy as jnp
from jax import lax
from jax.experimental import pallas as pl
from jax.experimental.pallas import tpu as pltpu
from jax.sharding import Mesh
from jax.sharding import PartitionSpec as P

EPS = 0.05
LOG2E = 1.4426950408889634
LN2 = 0.6931471805599453
BF16 = jnp.bfloat16
F32 = jnp.float32
PIECE = 256
EXTRA = 16
DEPTH = 256
GROUP = 16
LOW = -1e30
VMEM_LIMIT = 24 * 1024 * 1024


def split3(v):
    high = v.astype(BF16).astype(F32)
    rest = v - high
    mid = rest.astype(BF16).astype(F32)
    return high, mid, rest - mid


def wide(ref, row):
    pair = ref[pl.ds(row, 2), :]
    return jnp.concatenate([pair[0:1], pair[1:2]], axis=1)


def put_wide(ref, row, v):
    ref[pl.ds(row, 1), :] = v[:, 0:128]
    ref[pl.ds(row + 1, 1), :] = v[:, 128:256]


def rows_of(terms, count, width):
    row = lax.broadcasted_iota(jnp.int32, (count, width), 0)
    out = jnp.zeros((count, width), F32)
    for index, term in enumerate(terms):
        out = jnp.where(row == index, term, out)
    return out


def pack_kernel(x_ref, y_ref, la_ref, lb_ref, g_ref, xo_ref, yo_ref):
    feat = x_ref.shape[0]
    la = wide(la_ref, 0) * LOG2E
    y = y_ref[...].astype(F32)
    ny = jnp.sum(y * y, axis=0, keepdims=True)
    mine = lax.axis_index("y") * 8 + lax.axis_index("zh") * 2 + lax.axis_index("zl")
    g = wide(g_ref, 2 * mine)
    own = (wide(lb_ref, 0) + (g - ny / feat) / EPS) * LOG2E
    one = jnp.ones((1, PIECE), F32)
    xo_ref[0:feat, :] = x_ref[...]
    xo_ref[feat : feat + EXTRA, :] = rows_of(split3(la) + (one, one, one), EXTRA, PIECE).astype(BF16)
    yo_ref[0:feat, :] = y_ref[...]
    yo_ref[feat : feat + EXTRA, :] = rows_of(split3(own) + (one, one, one), EXTRA, PIECE).astype(BF16)


def left_side(ref, scale, term):
    feat = ref.shape[0] - EXTRA
    zero = jnp.zeros((1, PIECE), F32)
    extra = rows_of((zero, zero, zero) + split3(term), DEPTH - 3 * feat, PIECE)
    parts = split3(ref[0:feat, :].astype(F32) * scale)
    return jnp.transpose(jnp.concatenate(parts + (extra,), axis=0)).astype(BF16)


def right_side(ref, p):
    feat = ref.shape[1] - EXTRA
    v = ref[p, 0:feat, :]
    extra = ref[p, feat : feat + EXTRA, :]
    fill = jnp.zeros((DEPTH - 3 * feat - EXTRA, PIECE), BF16)
    return jnp.concatenate([v, v, v, extra, fill], axis=0)


def own_term(ref):
    feat = ref.shape[0] - EXTRA
    row = lax.broadcasted_iota(jnp.int32, (EXTRA, PIECE), 0)
    extra = ref[feat : feat + EXTRA, :].astype(F32)
    return jnp.sum(jnp.where(row < 3, extra, 0.0), axis=0, keepdims=True)


def norm(ref):
    feat = ref.shape[0] - EXTRA
    v = ref[0:feat, :].astype(F32)
    return jnp.sum(v * v, axis=0, keepdims=True)


def fold(s, how):
    return how(s.reshape(s.shape[0] // 8, 8, s.shape[1]), axis=0)


CHUNK = 1024
SAMPLE = 64
STEP = 4
LIFT = 80.0
ROOM = 110.0


def sweep(fill, a_ref, r_ref, top_ref, peak_ref, acc_ref):
    n, tiles = a_ref.shape[0], r_ref.shape[0]

    def dot(first, count, right):
        return jnp.dot(a_ref[first : first + count, :], right, preferred_element_type=F32)

    def sample(t):
        return jnp.max(dot(0, SAMPLE, right_side(r_ref, t)), axis=0, keepdims=True) + LIFT

    def chunk(c, right, top, acc, peak):
        s = dot(c * CHUNK, CHUNK, right)
        if peak is not None:
            peak = jnp.maximum(peak, fold(s, jnp.max))
        return acc + fold(jnp.exp2(s - top), jnp.sum), peak

    def keep(t, top, acc, peak):
        top_ref[t] = jnp.broadcast_to(top, (8, PIECE))
        acc_ref[t] = acc
        if peak is not None:
            peak_ref[t] = peak

    def total(t, top, peak):
        right = right_side(r_ref, t)
        acc = jnp.zeros((8, PIECE), F32)
        for c in range(n // CHUNK):
            acc, peak = chunk(c, right, top, acc, peak)
        keep(t, top, acc, peak)

    low = jnp.full((8, PIECE), LOW, F32)
    fill(0)
    tops = [sample(t) for t in range(STEP)]
    state = [(jnp.zeros((8, PIECE), F32), low)] * STEP
    for c in range(n // CHUNK):
        if (c + 1) * CHUNK < n:
            fill(c + 1)
        state = [chunk(c, right_side(r_ref, t), tops[t], *state[t]) for t in range(STEP)]
    for t in range(STEP):
        keep(t, tops[t], *state[t])

    def body(u, top):
        for t in range(STEP):
            later = sample(jnp.minimum(STEP * u + t + 1, tiles - 1))
            total(STEP * u + t, top, low)
            top = later
        return top

    lax.fori_loop(1, tiles // STEP, body, sample(STEP))

    over = jnp.max(jnp.max(peak_ref[...] - top_ref[...], axis=1), axis=1, keepdims=True) > ROOM
    bits = jnp.exp2(lax.broadcasted_iota(jnp.int32, (tiles, 1), 0).astype(F32))
    mask = jnp.sum(jnp.where(over, bits, 0.0)).astype(jnp.int32)

    @pl.when(mask > 0)
    def _():
        def again(t, carry):
            @pl.when((mask >> t) & 1 == 1)
            def _():
                total(t, jnp.max(peak_ref[t], axis=0, keepdims=True), None)

            return carry

        lax.fori_loop(0, tiles, again, 0)


def lse_of(top_ref, acc_ref, t):
    return top_ref[t, 0:1, :] + jnp.log2(jnp.sum(acc_ref[t], axis=0, keepdims=True))


def row_kernel(*refs, scale):
    xs, ys = refs[0:4], refs[4:8]
    out_ref, x_ref, y_ref, a_ref, top_ref, peak_ref, acc_ref = refs[8:]
    xi, zl, core = lax.axis_index("x"), lax.axis_index("zl"), lax.axis_index("c")
    yi, zh = lax.axis_index("y"), lax.axis_index("zh")
    for k in range(4):
        for j in range(4):
            x_ref[((zl + k // 2) % 2 * 4 + (xi + 4 - j) % 4) * 2 + (core + k % 2) % 2] = xs[k][j]
            y_ref[(yi + 4 - k) % 4 * 4 + (zh + 4 - j) % 4] = ys[k][j]

    def fill(c):
        for j in range(CHUNK // PIECE):
            left = left_side(ys[c].at[j], scale, own_term(ys[c].at[j]))
            a_ref[(4 * c + j) * PIECE : (4 * c + j + 1) * PIECE, :] = left

    sweep(fill, a_ref, x_ref, top_ref, peak_ref, acc_ref)
    for p in range(GROUP):
        put_wide(out_ref.at[0], 2 * p, lse_of(top_ref, acc_ref, p))
    lse = out_ref[0]
    for d in range(1, out_ref.shape[0]):
        out_ref[d] = lse


def col_kernel(x_ref, y_ref, lse_ref, f_ref, out_ref, a_ref, top_ref, peak_ref, acc_ref, fs_ref, ny_ref, *, scale):
    feat = x_ref.shape[1] - EXTRA
    part = lse_ref[...]
    top = jnp.max(part, axis=0)
    whole = top + jnp.log2(jnp.sum(jnp.exp2(part - top[None]), axis=0))

    def fill(c):
        for p in range(c * CHUNK // PIECE, (c + 1) * CHUNK // PIECE):
            lse = jnp.concatenate([whole[2 * p : 2 * p + 1], whole[2 * p + 1 : 2 * p + 2]], axis=1)
            put_wide(fs_ref, 2 * p, norm(x_ref.at[p]) / feat - (EPS * LN2) * lse)
            put_wide(ny_ref, 2 * p, norm(y_ref.at[p]) * (LOG2E / (feat * EPS)))
            left = left_side(x_ref.at[p], scale, own_term(x_ref.at[p]) - lse)
            a_ref[p * PIECE : (p + 1) * PIECE, :] = left

    sweep(fill, a_ref, y_ref, top_ref, peak_ref, acc_ref)
    f_ref[...] = fs_ref[pl.ds(pl.multiple_of(lax.axis_index("zl") * GROUP, GROUP), GROUP), :]
    for p in range(GROUP):
        put_wide(out_ref.at[0], 2 * p, lse_of(top_ref, acc_ref, p))
    u = out_ref[0] - ny_ref[...]
    for d in range(out_ref.shape[0]):
        out_ref[d] = u


def merge_kernel(u_ref, out_ref):
    u = u_ref[...]
    top = jnp.max(u, axis=0)
    out_ref[...] = (top + jnp.log2(jnp.sum(jnp.exp2(u - top[None]), axis=0))) * (-EPS * LN2)


def last_kernel(mine_ref, other_ref, out_ref):
    first = lax.axis_index("zl") == 0
    mine, other = mine_ref[...], other_ref[...]
    even, odd = jnp.where(first, mine, other), jnp.where(first, other, mine)
    for p in range(GROUP):
        out_ref[4 * p : 4 * p + 2, :] = even[2 * p : 2 * p + 2]
        out_ref[4 * p + 2 : 4 * p + 4, :] = odd[2 * p : 2 * p + 2]


def call(kernel, outs, args, scratch=(), name=None, vmem_limit=VMEM_LIMIT):
    vmem = pl.BlockSpec(memory_space=pltpu.VMEM)
    return pl.pallas_call(
        kernel,
        out_shape=outs,
        in_specs=[vmem] * len(args),
        out_specs=jax.tree.map(lambda _: vmem, outs),
        scratch_shapes=list(scratch),
        compiler_params=pltpu.CompilerParams(vmem_limit_bytes=vmem_limit),
        name=name,
    )(*args)


def ring(v, axis):
    return [v] + [lax.ppermute(v, axis, [(i, (i + k) % 4) for i in range(4)]) for k in (1, 2, 3)]


def local(x_feat, y_feat, log_a, log_b, g_init):
    feat, piece = x_feat.shape
    scale = 2.0 * LOG2E / (feat * EPS)
    shape = jax.ShapeDtypeStruct
    depth = feat + EXTRA
    n = GROUP * piece
    xo, yo = call(
        pack_kernel,
        [shape((depth, piece), BF16), shape((depth, piece), BF16)],
        (
            x_feat,
            y_feat,
            log_a.reshape(-1, 128),
            log_b.reshape(-1, 128),
            g_init.reshape(-1, 128),
        ),
        name="pack",
        vmem_limit=60 * 1024 * 1024,
    )
    ya = ring(yo, "zh")
    xa = ring(xo, "x")
    ya, xa = lax.optimization_barrier((ya, xa))
    yb = ring(jnp.stack(ya), "y")
    pair = [(0, 1), (1, 0)]
    xb = [jnp.stack(xa)]
    xb.append(lax.ppermute(xb[0], "c", pair))
    xb.append(lax.ppermute(xb[0], "zl", pair))
    xb.append(lax.ppermute(xb[2], "c", pair))
    left = pltpu.VMEM((n, DEPTH), BF16)
    stats = [pltpu.VMEM((GROUP, 8, piece), F32)] * 3
    pieces = shape((GROUP, depth, piece), BF16)
    spread = shape((GROUP, n // 128, 128), F32)
    lse, xs, ys = call(
        functools.partial(row_kernel, scale=scale),
        [spread, pieces, pieces],
        (*xb, *yb),
        [left] + stats,
        name="row_pass",
    )
    parts = lax.all_to_all(lse, ("zl", "x", "c"), 0, 0)
    f, u = call(
        functools.partial(col_kernel, scale=scale),
        [shape((n // 256, 128), F32), spread],
        (xs, ys, parts),
        [left] + stats + [pltpu.VMEM((n // 128, 128), F32)] * 2,
        name="col_pass",
    )
    u = lax.all_to_all(u, ("y", "zh"), 0, 0)
    mine = call(merge_kernel, shape((n // 128, 128), F32), (u,), name="merge")
    other = lax.ppermute(mine, "zl", [(0, 1), (1, 0)])
    g = call(last_kernel, shape((n // 64, 128), F32), (mine, other), name="last")
    return f.reshape(n // 2), g.reshape(2 * n)


def solution(mesh):
    inner = Mesh(mesh.devices.reshape(4, 4, 2, 4, 2), ("y", "zh", "zl", "x", "c"))
    rows, cols = ("y", "zh", "zl"), ("x", "c")
    placed = (P(None, rows + cols), P(None, cols + rows), P(rows + cols), P(cols + rows), P(cols))
    return jax.shard_map(
        local, mesh=inner, in_specs=placed, out_specs=(P(rows), P(cols)), check_vma=False
    )
```

```python
import functools

import jax
import jax.numpy as jnp
from jax import lax
from jax.experimental import pallas as pl
from jax.experimental.pallas import tpu as pltpu
from jax.sharding import Mesh
from jax.sharding import PartitionSpec as P

EPS = 0.05
LOG2E = 1.4426950408889634
LN2 = 0.6931471805599453
BF16 = jnp.bfloat16
F32 = jnp.float32
PIECE = 256
EXTRA = 16
DEPTH = 256
GROUP = 16
LOW = -1e30
VMEM_LIMIT = 24 * 1024 * 1024


def split3(v):
    high = v.astype(BF16).astype(F32)
    rest = v - high
    mid = rest.astype(BF16).astype(F32)
    return high, mid, rest - mid


def wide(ref, row):
    pair = ref[pl.ds(row, 2), :]
    return jnp.concatenate([pair[0:1], pair[1:2]], axis=1)


def put_wide(ref, row, v):
    ref[pl.ds(row, 1), :] = v[:, 0:128]
    ref[pl.ds(row + 1, 1), :] = v[:, 128:256]


def rows_of(terms, count, width):
    row = lax.broadcasted_iota(jnp.int32, (count, width), 0)
    out = jnp.zeros((count, width), F32)
    for index, term in enumerate(terms):
        out = jnp.where(row == index, term, out)
    return out


def pack_kernel(x_ref, y_ref, la_ref, lb_ref, g_ref, xo_ref, yo_ref):
    feat = x_ref.shape[0]
    la = wide(la_ref, 0) * LOG2E
    y = y_ref[...].astype(F32)
    ny = jnp.sum(y * y, axis=0, keepdims=True)
    mine = lax.axis_index("y") * 8 + lax.axis_index("zh") * 2 + lax.axis_index("zl")
    g = wide(g_ref, 2 * mine)
    own = (wide(lb_ref, 0) + (g - ny / feat) / EPS) * LOG2E
    one = jnp.ones((1, PIECE), F32)
    xo_ref[0:feat, :] = x_ref[...]
    xo_ref[feat : feat + EXTRA, :] = rows_of(split3(la) + (one, one, one), EXTRA, PIECE).astype(BF16)
    yo_ref[0:feat, :] = y_ref[...]
    yo_ref[feat : feat + EXTRA, :] = rows_of(split3(own) + (one, one, one), EXTRA, PIECE).astype(BF16)


def left_side(ref, scale, term):
    feat = ref.shape[0] - EXTRA
    zero = jnp.zeros((1, PIECE), F32)
    extra = rows_of((zero, zero, zero) + split3(term), DEPTH - 3 * feat, PIECE)
    parts = split3(ref[0:feat, :].astype(F32) * scale)
    return jnp.transpose(jnp.concatenate(parts + (extra,), axis=0)).astype(BF16)


def right_side(ref, p):
    feat = ref.shape[1] - EXTRA
    v = ref[p, 0:feat, :]
    extra = ref[p, feat : feat + EXTRA, :]
    fill = jnp.zeros((DEPTH - 3 * feat - EXTRA, PIECE), BF16)
    return jnp.concatenate([v, v, v, extra, fill], axis=0)


def own_term(ref):
    feat = ref.shape[0] - EXTRA
    row = lax.broadcasted_iota(jnp.int32, (EXTRA, PIECE), 0)
    extra = ref[feat : feat + EXTRA, :].astype(F32)
    return jnp.sum(jnp.where(row < 3, extra, 0.0), axis=0, keepdims=True)


def norm(ref):
    feat = ref.shape[0] - EXTRA
    v = ref[0:feat, :].astype(F32)
    return jnp.sum(v * v, axis=0, keepdims=True)


def fold(s, how):
    return how(s.reshape(s.shape[0] // 8, 8, s.shape[1]), axis=0)


CHUNK = 1024
SAMPLE = 64
STEP = 8
LIFT = 80.0
ROOM = 110.0


def sweep(fill, a_ref, r_ref, top_ref, peak_ref, acc_ref):
    n, tiles = a_ref.shape[0], r_ref.shape[0]

    def dot(first, count, right):
        return jnp.dot(a_ref[first : first + count, :], right, preferred_element_type=F32)

    def sample(t):
        return jnp.max(dot(0, SAMPLE, right_side(r_ref, t)), axis=0, keepdims=True) + LIFT

    def chunk(c, right, top, acc, peak):
        s = dot(c * CHUNK, CHUNK, right)
        if peak is not None:
            peak = jnp.maximum(peak, fold(s, jnp.max))
        return acc + fold(jnp.exp2(s - top), jnp.sum), peak

    def keep(t, top, acc, peak):
        top_ref[t] = jnp.broadcast_to(top, (8, PIECE))
        acc_ref[t] = acc
        if peak is not None:
            peak_ref[t] = peak

    def total(t, top, peak):
        right = right_side(r_ref, t)
        acc = jnp.zeros((8, PIECE), F32)
        for c in range(n // CHUNK):
            acc, peak = chunk(c, right, top, acc, peak)
        keep(t, top, acc, peak)

    low = jnp.full((8, PIECE), LOW, F32)
    fill(0)
    tops = [sample(t) for t in range(STEP)]
    state = [(jnp.zeros((8, PIECE), F32), low)] * STEP
    for c in range(n // CHUNK):
        if (c + 1) * CHUNK < n:
            fill(c + 1)
        state = [chunk(c, right_side(r_ref, t), tops[t], *state[t]) for t in range(STEP)]
    for t in range(STEP):
        keep(t, tops[t], *state[t])

    def body(u, top):
        for t in range(STEP):
            later = sample(jnp.minimum(STEP * u + t + 1, tiles - 1))
            total(STEP * u + t, top, low)
            top = later
        return top

    lax.fori_loop(1, tiles // STEP, body, sample(STEP))

    over = jnp.max(jnp.max(peak_ref[...] - top_ref[...], axis=1), axis=1, keepdims=True) > ROOM
    bits = jnp.exp2(lax.broadcasted_iota(jnp.int32, (tiles, 1), 0).astype(F32))
    mask = jnp.sum(jnp.where(over, bits, 0.0)).astype(jnp.int32)

    @pl.when(mask > 0)
    def _():
        def again(t, carry):
            @pl.when((mask >> t) & 1 == 1)
            def _():
                total(t, jnp.max(peak_ref[t], axis=0, keepdims=True), None)

            return carry

        lax.fori_loop(0, tiles, again, 0)


def lse_of(top_ref, acc_ref, t):
    return top_ref[t, 0:1, :] + jnp.log2(jnp.sum(acc_ref[t], axis=0, keepdims=True))


def row_kernel(*refs, scale):
    xs, ys = refs[0:4], refs[4:8]
    out_ref, x_ref, y_ref, a_ref, top_ref, peak_ref, acc_ref = refs[8:]
    xi, zl, core = lax.axis_index("x"), lax.axis_index("zl"), lax.axis_index("c")
    yi, zh = lax.axis_index("y"), lax.axis_index("zh")
    for k in range(4):
        for j in range(4):
            x_ref[((zl + k // 2) % 2 * 4 + (xi + 4 - j) % 4) * 2 + (core + k % 2) % 2] = xs[k][j]
            y_ref[(yi + 4 - k) % 4 * 4 + (zh + 4 - j) % 4] = ys[k][j]

    def fill(c):
        for j in range(CHUNK // PIECE):
            left = left_side(ys[c].at[j], scale, own_term(ys[c].at[j]))
            a_ref[(4 * c + j) * PIECE : (4 * c + j + 1) * PIECE, :] = left

    sweep(fill, a_ref, x_ref, top_ref, peak_ref, acc_ref)
    for p in range(GROUP):
        put_wide(out_ref.at[0], 2 * p, lse_of(top_ref, acc_ref, p))
    lse = out_ref[0]
    for d in range(1, out_ref.shape[0]):
        out_ref[d] = lse


def col_kernel(x_ref, y_ref, lse_ref, f_ref, out_ref, a_ref, top_ref, peak_ref, acc_ref, fs_ref, ny_ref, *, scale):
    feat = x_ref.shape[1] - EXTRA
    part = lse_ref[...]
    top = jnp.max(part, axis=0)
    whole = top + jnp.log2(jnp.sum(jnp.exp2(part - top[None]), axis=0))

    def fill(c):
        for p in range(c * CHUNK // PIECE, (c + 1) * CHUNK // PIECE):
            lse = jnp.concatenate([whole[2 * p : 2 * p + 1], whole[2 * p + 1 : 2 * p + 2]], axis=1)
            put_wide(fs_ref, 2 * p, norm(x_ref.at[p]) / feat - (EPS * LN2) * lse)
            put_wide(ny_ref, 2 * p, norm(y_ref.at[p]) * (LOG2E / (feat * EPS)))
            left = left_side(x_ref.at[p], scale, own_term(x_ref.at[p]) - lse)
            a_ref[p * PIECE : (p + 1) * PIECE, :] = left

    sweep(fill, a_ref, y_ref, top_ref, peak_ref, acc_ref)
    f_ref[...] = fs_ref[pl.ds(pl.multiple_of(lax.axis_index("zl") * GROUP, GROUP), GROUP), :]
    for p in range(GROUP):
        put_wide(out_ref.at[0], 2 * p, lse_of(top_ref, acc_ref, p))
    u = out_ref[0] - ny_ref[...]
    for d in range(out_ref.shape[0]):
        out_ref[d] = u


def merge_kernel(u_ref, out_ref):
    u = u_ref[...]
    top = jnp.max(u, axis=0)
    out_ref[...] = (top + jnp.log2(jnp.sum(jnp.exp2(u - top[None]), axis=0))) * (-EPS * LN2)


def last_kernel(mine_ref, other_ref, out_ref):
    first = lax.axis_index("zl") == 0
    mine, other = mine_ref[...], other_ref[...]
    even, odd = jnp.where(first, mine, other), jnp.where(first, other, mine)
    for p in range(GROUP):
        out_ref[4 * p : 4 * p + 2, :] = even[2 * p : 2 * p + 2]
        out_ref[4 * p + 2 : 4 * p + 4, :] = odd[2 * p : 2 * p + 2]


def call(kernel, outs, args, scratch=(), name=None, vmem_limit=VMEM_LIMIT):
    vmem = pl.BlockSpec(memory_space=pltpu.VMEM)
    return pl.pallas_call(
        kernel,
        out_shape=outs,
        in_specs=[vmem] * len(args),
        out_specs=jax.tree.map(lambda _: vmem, outs),
        scratch_shapes=list(scratch),
        compiler_params=pltpu.CompilerParams(vmem_limit_bytes=vmem_limit),
        name=name,
    )(*args)


def ring(v, axis):
    return [v] + [lax.ppermute(v, axis, [(i, (i + k) % 4) for i in range(4)]) for k in (1, 2, 3)]


def local(x_feat, y_feat, log_a, log_b, g_init):
    feat, piece = x_feat.shape
    scale = 2.0 * LOG2E / (feat * EPS)
    shape = jax.ShapeDtypeStruct
    depth = feat + EXTRA
    n = GROUP * piece
    xo, yo = call(
        pack_kernel,
        [shape((depth, piece), BF16), shape((depth, piece), BF16)],
        (
            x_feat,
            y_feat,
            log_a.reshape(-1, 128),
            log_b.reshape(-1, 128),
            g_init.reshape(-1, 128),
        ),
        name="pack",
        vmem_limit=60 * 1024 * 1024,
    )
    ya = ring(yo, "zh")
    xa = ring(xo, "x")
    ya, xa = lax.optimization_barrier((ya, xa))
    yb = ring(jnp.stack(ya), "y")
    pair = [(0, 1), (1, 0)]
    xb = [jnp.stack(xa)]
    xb.append(lax.ppermute(xb[0], "c", pair))
    xb.append(lax.ppermute(xb[0], "zl", pair))
    xb.append(lax.ppermute(xb[2], "c", pair))
    left = pltpu.VMEM((n, DEPTH), BF16)
    stats = [pltpu.VMEM((GROUP, 8, piece), F32)] * 3
    pieces = shape((GROUP, depth, piece), BF16)
    spread = shape((GROUP, n // 128, 128), F32)
    lse, xs, ys = call(
        functools.partial(row_kernel, scale=scale),
        [spread, pieces, pieces],
        (*xb, *yb),
        [left] + stats,
        name="row_pass",
    )
    parts = lax.all_to_all(lse, ("zl", "x", "c"), 0, 0)
    f, u = call(
        functools.partial(col_kernel, scale=scale),
        [shape((n // 256, 128), F32), spread],
        (xs, ys, parts),
        [left] + stats + [pltpu.VMEM((n // 128, 128), F32)] * 2,
        name="col_pass",
    )
    u = lax.all_to_all(u, ("y", "zh"), 0, 0)
    mine = call(merge_kernel, shape((n // 128, 128), F32), (u,), name="merge")
    other = lax.ppermute(mine, "zl", [(0, 1), (1, 0)])
    g = call(last_kernel, shape((n // 64, 128), F32), (mine, other), name="last")
    return f.reshape(n // 2), g.reshape(2 * n)


def solution(mesh):
    inner = Mesh(mesh.devices.reshape(4, 4, 2, 4, 2), ("y", "zh", "zl", "x", "c"))
    rows, cols = ("y", "zh", "zl"), ("x", "c")
    placed = (P(None, rows + cols), P(None, cols + rows), P(rows + cols), P(cols + rows), P(cols))
    return jax.shard_map(
        local, mesh=inner, in_specs=placed, out_specs=(P(rows), P(cols)), check_vma=False
    )
```

```python
import functools

import jax
import jax.numpy as jnp
from jax import lax
from jax.experimental import pallas as pl
from jax.experimental.pallas import tpu as pltpu
from jax.sharding import Mesh
from jax.sharding import PartitionSpec as P

EPS = 0.05
LOG2E = 1.4426950408889634
LN2 = 0.6931471805599453
BF16 = jnp.bfloat16
F32 = jnp.float32
PIECE = 256
EXTRA = 8
DEPTH = 256
GROUP = 16
LOW = -1e30
VMEM_LIMIT = 24 * 1024 * 1024


def split3(v):
    high = v.astype(BF16).astype(F32)
    rest = v - high
    mid = rest.astype(BF16).astype(F32)
    return high, mid, rest - mid


def wide(ref, row):
    pair = ref[pl.ds(row, 2), :]
    return jnp.concatenate([pair[0:1], pair[1:2]], axis=1)


def put_wide(ref, row, v):
    ref[pl.ds(row, 1), :] = v[:, 0:128]
    ref[pl.ds(row + 1, 1), :] = v[:, 128:256]


def rows_of(terms, count, width):
    row = lax.broadcasted_iota(jnp.int32, (count, width), 0)
    out = jnp.zeros((count, width), F32)
    for index, term in enumerate(terms):
        out = jnp.where(row == index, term, out)
    return out


def pack_kernel(x_ref, y_ref, la_ref, lb_ref, g_ref, xo_ref, yo_ref):
    feat = x_ref.shape[0]
    la = wide(la_ref, 0) * LOG2E
    y = y_ref[...].astype(F32)
    ny = jnp.sum(y * y, axis=0, keepdims=True)
    mine = lax.axis_index("y") * 8 + lax.axis_index("zh") * 2 + lax.axis_index("zl")
    g = wide(g_ref, 2 * mine)
    own = (wide(lb_ref, 0) + (g - ny / feat) / EPS) * LOG2E
    one = jnp.ones((1, PIECE), F32)
    x_extra = rows_of(split3(la) + (one, one, one), EXTRA, PIECE)
    y_extra = rows_of(split3(own) + (one, one, one), EXTRA, PIECE)
    xo_ref[...] = jnp.concatenate([x_ref[...].astype(F32), x_extra], axis=0).astype(BF16)
    yo_ref[...] = jnp.concatenate([y, y_extra], axis=0).astype(BF16)


def left_side(ref, scale, term):
    feat = ref.shape[0] - EXTRA
    zero = jnp.zeros((1, PIECE), F32)
    extra = rows_of((zero, zero, zero) + split3(term), DEPTH - 3 * feat, PIECE)
    parts = split3(ref[0:feat, :].astype(F32) * scale)
    return jnp.transpose(jnp.concatenate(parts + (extra,), axis=0)).astype(BF16)


def right_side(ref, p):
    feat = ref.shape[1] - EXTRA
    v = ref[p, 0:feat, :]
    extra = extra_rows(ref.at[p])
    fill = jnp.zeros((DEPTH - 3 * feat - EXTRA, PIECE), F32)
    return jnp.concatenate([v, v, v, jnp.concatenate([extra, fill], axis=0).astype(BF16)], axis=0)


def extra_rows(ref):
    return ref[...].astype(F32)[ref.shape[0] - EXTRA :, :]


def own_term(ref):
    row = lax.broadcasted_iota(jnp.int32, (EXTRA, PIECE), 0)
    return jnp.sum(jnp.where(row < 3, extra_rows(ref), 0.0), axis=0, keepdims=True)


def norm(ref):
    feat = ref.shape[0] - EXTRA
    v = ref[0:feat, :].astype(F32)
    return jnp.sum(v * v, axis=0, keepdims=True)


def fold(s, how):
    return how(s.reshape(s.shape[0] // 8, 8, s.shape[1]), axis=0)


CHUNK = 1024
SAMPLE = 64
STEP = 8
LIFT = 80.0
ROOM = 110.0


def sweep(fill, a_ref, r_ref, top_ref, peak_ref, acc_ref):
    n, tiles = a_ref.shape[0], r_ref.shape[0]

    def dot(first, count, right):
        return jnp.dot(a_ref[first : first + count, :], right, preferred_element_type=F32)

    def sample(t):
        return jnp.max(dot(0, SAMPLE, right_side(r_ref, t)), axis=0, keepdims=True) + LIFT

    def chunk(c, right, top, acc, peak):
        s = dot(c * CHUNK, CHUNK, right)
        if peak is not None:
            peak = jnp.maximum(peak, fold(s, jnp.max))
        return acc + fold(jnp.exp2(s - top), jnp.sum), peak

    def keep(t, top, acc, peak):
        top_ref[t] = jnp.broadcast_to(top, (8, PIECE))
        acc_ref[t] = acc
        if peak is not None:
            peak_ref[t] = peak

    def total(t, top, peak):
        right = right_side(r_ref, t)
        acc = jnp.zeros((8, PIECE), F32)
        for c in range(n // CHUNK):
            acc, peak = chunk(c, right, top, acc, peak)
        keep(t, top, acc, peak)

    low = jnp.full((8, PIECE), LOW, F32)
    fill(0)
    tops = [sample(t) for t in range(STEP)]
    state = [(jnp.zeros((8, PIECE), F32), low)] * STEP
    for c in range(n // CHUNK):
        if (c + 1) * CHUNK < n:
            fill(c + 1)
        state = [chunk(c, right_side(r_ref, t), tops[t], *state[t]) for t in range(STEP)]
    for t in range(STEP):
        keep(t, tops[t], *state[t])

    def body(u, top):
        for t in range(STEP):
            later = sample(jnp.minimum(STEP * u + t + 1, tiles - 1))
            total(STEP * u + t, top, low)
            top = later
        return top

    lax.fori_loop(1, tiles // STEP, body, sample(STEP))

    over = jnp.max(jnp.max(peak_ref[...] - top_ref[...], axis=1), axis=1, keepdims=True) > ROOM
    bits = jnp.exp2(lax.broadcasted_iota(jnp.int32, (tiles, 1), 0).astype(F32))
    mask = jnp.sum(jnp.where(over, bits, 0.0)).astype(jnp.int32)

    @pl.when(mask > 0)
    def _():
        def again(t, carry):
            @pl.when((mask >> t) & 1 == 1)
            def _():
                total(t, jnp.max(peak_ref[t], axis=0, keepdims=True), None)

            return carry

        lax.fori_loop(0, tiles, again, 0)


def lse_of(top_ref, acc_ref, t):
    return top_ref[t, 0:1, :] + jnp.log2(jnp.sum(acc_ref[t], axis=0, keepdims=True))


def row_kernel(*refs, scale):
    xs, ys = refs[0:4], refs[4:8]
    out_ref, x_ref, y_ref, a_ref, top_ref, peak_ref, acc_ref = refs[8:]
    xi, zl, core = lax.axis_index("x"), lax.axis_index("zl"), lax.axis_index("c")
    yi, zh = lax.axis_index("y"), lax.axis_index("zh")
    for k in range(4):
        for j in range(4):
            x_ref[((zl + k // 2) % 2 * 4 + (xi + 4 - j) % 4) * 2 + (core + k % 2) % 2] = xs[k][j]
            y_ref[(yi + 4 - k) % 4 * 4 + (zh + 4 - j) % 4] = ys[k][j]

    def fill(c):
        for j in range(CHUNK // PIECE):
            left = left_side(ys[c].at[j], scale, own_term(ys[c].at[j]))
            a_ref[(4 * c + j) * PIECE : (4 * c + j + 1) * PIECE, :] = left

    sweep(fill, a_ref, x_ref, top_ref, peak_ref, acc_ref)
    for p in range(GROUP):
        put_wide(out_ref.at[0], 2 * p, lse_of(top_ref, acc_ref, p))
    lse = out_ref[0]
    for d in range(1, out_ref.shape[0]):
        out_ref[d] = lse


def col_kernel(x_ref, y_ref, lse_ref, f_ref, out_ref, a_ref, top_ref, peak_ref, acc_ref, fs_ref, ny_ref, *, scale):
    feat = x_ref.shape[1] - EXTRA
    part = lse_ref[...]
    top = jnp.max(part, axis=0)
    whole = top + jnp.log2(jnp.sum(jnp.exp2(part - top[None]), axis=0))

    def fill(c):
        for p in range(c * CHUNK // PIECE, (c + 1) * CHUNK // PIECE):
            lse = jnp.concatenate([whole[2 * p : 2 * p + 1], whole[2 * p + 1 : 2 * p + 2]], axis=1)
            put_wide(fs_ref, 2 * p, norm(x_ref.at[p]) / feat - (EPS * LN2) * lse)
            put_wide(ny_ref, 2 * p, norm(y_ref.at[p]) * (LOG2E / (feat * EPS)))
            left = left_side(x_ref.at[p], scale, own_term(x_ref.at[p]) - lse)
            a_ref[p * PIECE : (p + 1) * PIECE, :] = left

    sweep(fill, a_ref, y_ref, top_ref, peak_ref, acc_ref)
    f_ref[...] = fs_ref[pl.ds(pl.multiple_of(lax.axis_index("zl") * GROUP, GROUP), GROUP), :]
    for p in range(GROUP):
        put_wide(out_ref.at[0], 2 * p, lse_of(top_ref, acc_ref, p))
    u = out_ref[0] - ny_ref[...]
    for d in range(out_ref.shape[0]):
        out_ref[d] = u


def merge_kernel(u_ref, out_ref):
    u = u_ref[...]
    top = jnp.max(u, axis=0)
    out_ref[...] = (top + jnp.log2(jnp.sum(jnp.exp2(u - top[None]), axis=0))) * (-EPS * LN2)


def last_kernel(mine_ref, other_ref, out_ref):
    first = lax.axis_index("zl") == 0
    mine, other = mine_ref[...], other_ref[...]
    even, odd = jnp.where(first, mine, other), jnp.where(first, other, mine)
    for p in range(GROUP):
        out_ref[4 * p : 4 * p + 2, :] = even[2 * p : 2 * p + 2]
        out_ref[4 * p + 2 : 4 * p + 4, :] = odd[2 * p : 2 * p + 2]


def call(kernel, outs, args, scratch=(), name=None, vmem_limit=VMEM_LIMIT):
    vmem = pl.BlockSpec(memory_space=pltpu.VMEM)
    return pl.pallas_call(
        kernel,
        out_shape=outs,
        in_specs=[vmem] * len(args),
        out_specs=jax.tree.map(lambda _: vmem, outs),
        scratch_shapes=list(scratch),
        compiler_params=pltpu.CompilerParams(vmem_limit_bytes=vmem_limit),
        name=name,
    )(*args)


def ring(v, axis):
    return [v] + [lax.ppermute(v, axis, [(i, (i + k) % 4) for i in range(4)]) for k in (1, 2, 3)]


def local(x_feat, y_feat, log_a, log_b, g_init):
    feat, piece = x_feat.shape
    scale = 2.0 * LOG2E / (feat * EPS)
    shape = jax.ShapeDtypeStruct
    depth = feat + EXTRA
    n = GROUP * piece
    xo, yo = call(
        pack_kernel,
        [shape((depth, piece), BF16), shape((depth, piece), BF16)],
        (
            x_feat,
            y_feat,
            log_a.reshape(-1, 128),
            log_b.reshape(-1, 128),
            g_init.reshape(-1, 128),
        ),
        name="pack",
        vmem_limit=60 * 1024 * 1024,
    )
    ya = ring(yo, "zh")
    xa = ring(xo, "x")
    ya, xa = lax.optimization_barrier((ya, xa))
    yb = ring(jnp.stack(ya), "y")
    pair = [(0, 1), (1, 0)]
    xb = [jnp.stack(xa)]
    xb.append(lax.ppermute(xb[0], "c", pair))
    xb.append(lax.ppermute(xb[0], "zl", pair))
    xb.append(lax.ppermute(xb[2], "c", pair))
    left = pltpu.VMEM((n, DEPTH), BF16)
    stats = [pltpu.VMEM((GROUP, 8, piece), F32)] * 3
    pieces = shape((GROUP, depth, piece), BF16)
    spread = shape((GROUP, n // 128, 128), F32)
    lse, xs, ys = call(
        functools.partial(row_kernel, scale=scale),
        [spread, pieces, pieces],
        (*xb, *yb),
        [left] + stats,
        name="row_pass",
    )
    parts = lax.all_to_all(lse, ("zl", "x", "c"), 0, 0)
    f, u = call(
        functools.partial(col_kernel, scale=scale),
        [shape((n // 256, 128), F32), spread],
        (xs, ys, parts),
        [left] + stats + [pltpu.VMEM((n // 128, 128), F32)] * 2,
        name="col_pass",
    )
    u = lax.all_to_all(u, ("y", "zh"), 0, 0)
    mine = call(merge_kernel, shape((n // 128, 128), F32), (u,), name="merge")
    other = lax.ppermute(mine, "zl", [(0, 1), (1, 0)])
    g = call(last_kernel, shape((n // 64, 128), F32), (mine, other), name="last")
    return f.reshape(n // 2), g.reshape(2 * n)


def solution(mesh):
    inner = Mesh(mesh.devices.reshape(4, 4, 2, 4, 2), ("y", "zh", "zl", "x", "c"))
    rows, cols = ("y", "zh", "zl"), ("x", "c")
    placed = (P(None, rows + cols), P(None, cols + rows), P(rows + cols), P(cols + rows), P(cols))
    return jax.shard_map(
        local, mesh=inner, in_specs=placed, out_specs=(P(rows), P(cols)), check_vma=False
    )
```
